512 devices in a mesh: dp: 128 (over z, y, core), tp: 4 (over x).
Axes of the slice: x: 4, y: 8, z: 8, core: 2. Of those that a mesh axis runs over, the one named last changes fastest.
Arguments:
- queries: bfloat16 [2, 128, 8192], P(None, 'dp', 'tp'), may hold values from -8 to 8
- new_token_keys: bfloat16 [2, 128, 512], P(None, 'dp', 'tp'), may hold values from -6 to 6
- new_token_values: bfloat16 [2, 128, 512], P(None, 'dp', 'tp'), may hold values from -6 to 6
- key_pool: bfloat16 [8192, 128, 512], P('dp', None, 'tp'), may hold values from -8 to 8
- value_pool: bfloat16 [8192, 128, 512], P('dp', None, 'tp'), may hold values from -6 to 6
- block_list: int32 [2, 4096, 2], P(None, ('dp', 'tp')), may hold values from 0 to 127, as said below
- context_len: int32 [2, 128], P(None, 'dp'), may hold values from 1 to 4096, as said below
Outputs:
- attn_out: bfloat16 [2, 128, 8192], P(None, 'dp', 'tp')
The draws below stay inside these ranges and needn't reach their ends.
Inputs may be any that keep to these rules, and one draw needn't show every extreme that they name: `block_list`: each entry is (holder rank, pool slot). Every slot of every holder holds exactly one block of one micro-batch. On one holder, the blocks of one rank's requests over both micro-batches number 0 or 2; the bound 2 is also reached within a single micro-batch. Cached tokens, the new token aside. For every rank and micro-batch, ceil(context_len / 128) summed over the rank's 1 request is 32.
All inputs are finite; a program needn't handle non-finite values.
Results may differ from the reference program's by a relative error of at most 0.011.
Values may be sent and summed in bfloat16 or wider, within the bound.
No kernel may reach another device: no remote copies, remote signals or barrier semaphores. Data moves between devices by JAX's collectives and lax.ppermute only.
A program may use at most 64 MiB of HBM per device.

```python
import math
import jax
import jax.numpy as jnp
from jax import lax

QUERY_HEADS = 64
KEY_VALUE_HEADS = 4
HEAD_SIZE = 128
BLOCK_TOKENS = 128
SLOTS = 64
MICRO_BATCHES = 2
RANK_REQUESTS = 1
BATCH_REQUESTS = 128
POOL_SLOTS = 8192
N_DP = 128


def layout(key):
    per_rank = SLOTS // 2
    capacity = max(2, SLOTS // N_DP)
    groups = SLOTS // capacity
    row_total = MICRO_BATCHES * N_DP
    cut_key, tail_key, pick_key, group_key, offset_key, order_key = jax.random.split(key, 6)

    def cuts_for(row_key):
        points = jnp.sort(jax.random.permutation(row_key, per_rank - 1)[:RANK_REQUESTS - 1] + 1).astype(jnp.int32)
        boundary = jnp.concatenate([jnp.zeros((1,), jnp.int32), points, jnp.full((1,), per_rank, jnp.int32)])
        return boundary[1:] - boundary[:-1]
    counts = jax.vmap(cuts_for)(jax.random.split(cut_key, row_total))
    tail_tokens = jax.random.randint(tail_key, (row_total, RANK_REQUESTS), 1, BLOCK_TOKENS + 1)
    chosen = jax.random.randint(pick_key, (), 0, row_total)
    forced = (jnp.arange(row_total, dtype=jnp.int32) == chosen)[:, None]
    leading = (jnp.arange(RANK_REQUESTS, dtype=jnp.int32) == 0)[None, :]
    counts = jnp.where(forced, jnp.where(leading, per_rank - RANK_REQUESTS + 1, 1), counts)
    tail_tokens = jnp.where(forced, jnp.where(leading, BLOCK_TOKENS, 1), tail_tokens)
    lengths = ((counts - 1) * BLOCK_TOKENS + tail_tokens).astype(jnp.int32)
    slot_group = jax.random.permutation(group_key, SLOTS) // capacity
    shuffled = jax.random.permutation(offset_key, N_DP).astype(jnp.int32)
    rank_of = jnp.argsort(shuffled, stable=True).astype(jnp.int32)
    candidates = jnp.arange(N_DP, dtype=jnp.int32)
    score = jnp.where(candidates == 1, -2, jnp.where(candidates == N_DP // 2, -1, rank_of))
    offsets = jnp.argsort(score, stable=True).astype(jnp.int32)[:groups]
    slot_offset = offsets[slot_group]

    def order_for(row_key):
        rank_key, pair_key = jax.random.split(row_key)
        ranking = jax.random.permutation(rank_key, SLOTS)
        pair_groups = jax.random.permutation(pair_key, groups)[:2]
        tier_rank = jnp.where(slot_group == pair_groups[0], 0, jnp.where(slot_group == pair_groups[1], 2, 1))
        return jnp.argsort(tier_rank * SLOTS + ranking, stable=True).astype(jnp.int32)
    orders = jax.vmap(order_for)(jax.random.split(order_key, N_DP))
    holders = (jnp.arange(N_DP, dtype=jnp.int32)[:, None] + slot_offset[orders]) % N_DP
    slot_ids = jnp.transpose(orders.reshape(N_DP, MICRO_BATCHES, per_rank), (1, 0, 2))
    holder_ids = jnp.transpose(holders.reshape(N_DP, MICRO_BATCHES, per_rank), (1, 0, 2))
    block_list = jnp.stack([holder_ids, slot_ids], axis=-1).reshape(MICRO_BATCHES, N_DP * per_rank, 2).astype(jnp.int32)
    return (block_list, lengths.reshape(MICRO_BATCHES, N_DP * RANK_REQUESTS))


def draw_block_list(key, part):
    tables = layout(key)
    return tables[0]


def draw_context_len(key, part):
    tables = layout(key)
    return tables[1]


def draw_queries(key, part):
    key = jax.random.fold_in(key, 1)
    random_seed_key = jax.random.fold_in(key, 1)
    value_entries = jax.random.normal(random_seed_key, (MICRO_BATCHES, BATCH_REQUESTS, QUERY_HEADS, HEAD_SIZE))
    return jnp.clip(value_entries, -8.0, 8.0).reshape(MICRO_BATCHES, BATCH_REQUESTS, QUERY_HEADS * HEAD_SIZE).astype(jnp.bfloat16)


def draw_key_pool(key, part):
    key = jax.random.fold_in(key, 2)
    random_seed_key = jax.random.fold_in(key, 1)
    value_entries = jax.random.normal(random_seed_key, (POOL_SLOTS, BLOCK_TOKENS, KEY_VALUE_HEADS, HEAD_SIZE))
    return jnp.clip(value_entries, -8.0, 8.0).reshape(POOL_SLOTS, BLOCK_TOKENS, KEY_VALUE_HEADS * HEAD_SIZE).astype(jnp.bfloat16)


def steps_of(rng, extent, cuts, low, top_value):
    loudness, own = 1.0, jax.random.fold_in(rng, 6)
    for axis_at, blocks in cuts:
        steps = jnp.exp(jax.random.uniform(jax.random.fold_in(own, axis_at), (blocks,), jnp.float32, low / len(cuts), top_value / len(cuts)))
        loudness = loudness * jnp.repeat(steps, extent[axis_at] // blocks).reshape([-1 if axis == axis_at else 1 for axis in range(len(extent))])
    return loudness


def gaussian(own_key, dims, width, limit, cuts=(), kind=jnp.bfloat16):
    array = jax.random.normal(own_key, dims, jnp.float32) * width
    if len(cuts) > 0:
        array = steps_of(own_key, dims, cuts, -0.22, 0.18) * array
    return jnp.clip(array, min=-limit, max=limit).astype(kind)


def setup_inputs(seed: int = 0) -> dict:
    keys = jax.random.split(jax.random.key(seed), 8)
    return {
        "queries": draw_queries(jax.random.fold_in(keys[7], 71), 0),
        "new_token_keys": gaussian(keys[1], (MICRO_BATCHES, BATCH_REQUESTS, KEY_VALUE_HEADS * HEAD_SIZE), 1.0, 6.0, ((1, 128), (2, 4))),
        "new_token_values": gaussian(keys[2], (MICRO_BATCHES, BATCH_REQUESTS, KEY_VALUE_HEADS * HEAD_SIZE), 1.0, 6.0, ((1, 128), (2, 4))),
        "key_pool": draw_key_pool(jax.random.fold_in(keys[7], 71), 0),
        "value_pool": gaussian(keys[4], (POOL_SLOTS, BLOCK_TOKENS, KEY_VALUE_HEADS * HEAD_SIZE), 1.0, 6.0, ((0, 128), (2, 4))),
        "block_list": draw_block_list(jax.random.fold_in(keys[7], 71), 0),
        "context_len": draw_context_len(jax.random.fold_in(keys[7], 71), 0),
    }


def block_terms(query_row_list, key_row_list, value_row_list, live_tokens):
    score_scale = query_row_list.shape[-1] ** -0.5
    scores = jnp.einsum("ekgd,ebkd->ekgb", query_row_list.astype(jnp.float32), key_row_list.astype(jnp.float32), precision=lax.Precision.HIGHEST) * score_scale
    live_mask = lax.broadcasted_iota(jnp.int32, scores.shape, 3) < live_tokens[:, None, None, None]
    scores = jnp.where(live_mask, scores, -1e30)
    peak_score = jnp.max(scores, axis=3)
    weight = jnp.where(live_mask, jnp.exp(scores - peak_score[..., None]), 0.0)
    weight_sum = jnp.sum(weight, axis=3)
    rounded = lax.optimization_barrier(weight.astype(jnp.bfloat16)).astype(jnp.float32)
    mixed_sum = jnp.einsum("ekgb,ebkd->ekgd", rounded, value_row_list.astype(jnp.float32), precision=lax.Precision.HIGHEST)
    partial_value = (mixed_sum / weight_sum[..., None]).astype(jnp.bfloat16)
    return partial_value, peak_score, weight_sum


def micro_batch(query_tile_block, fresh_key, fresh_value, key_pool, value_pool, block_rows, lengths):
    request_count, feature_width = query_tile_block.shape
    owner_ranks = request_count // RANK_REQUESTS
    per_rank = SLOTS // 2
    heads_per_group = QUERY_HEADS // KEY_VALUE_HEADS
    score_scale = HEAD_SIZE ** -0.5
    lengths = lengths.reshape(owner_ranks, RANK_REQUESTS)
    block_counts = (lengths + BLOCK_TOKENS - 1) // BLOCK_TOKENS
    block_ends = jnp.cumsum(block_counts, axis=1)
    block_starts = block_ends - block_counts
    position = jnp.arange(per_rank, dtype=jnp.int32)
    request = jnp.sum((position[None, :, None] >= block_ends[:, None, :]).astype(jnp.int32), axis=2)
    chosen = request[:, :, None] == jnp.arange(RANK_REQUESTS, dtype=jnp.int32)[None, None, :]
    first_block = jnp.sum(jnp.where(chosen, block_starts[:, None, :], 0), axis=2)
    span_tokens = jnp.sum(jnp.where(chosen, lengths[:, None, :], 0), axis=2)
    live_tokens = jnp.clip(span_tokens - (position[None, :] - first_block) * BLOCK_TOKENS, 0, BLOCK_TOKENS).reshape(-1).astype(jnp.int32)
    pool_rows = (block_rows[:, 0] * SLOTS + block_rows[:, 1]).astype(jnp.int32)
    query_ids = (jnp.arange(owner_ranks, dtype=jnp.int32)[:, None] * RANK_REQUESTS + request).reshape(-1).astype(jnp.int32)
    entries = owner_ranks * per_rank
    batch_rows = math.gcd(entries, 64)

    def one_batch(pieces):
        query_portion, pool_portion, token_piece = pieces
        query_row_list = jnp.take(query_tile_block, query_portion, axis=0).reshape(batch_rows, KEY_VALUE_HEADS, heads_per_group, HEAD_SIZE)
        key_row_list = jnp.take(key_pool, pool_portion, axis=0).reshape(batch_rows, BLOCK_TOKENS, KEY_VALUE_HEADS, HEAD_SIZE)
        value_row_list = jnp.take(value_pool, pool_portion, axis=0).reshape(batch_rows, BLOCK_TOKENS, KEY_VALUE_HEADS, HEAD_SIZE)
        return block_terms(query_row_list, key_row_list, value_row_list, token_piece)

    partial_value, peak_score, weight_sum = lax.map(one_batch, (query_ids.reshape(-1, batch_rows), pool_rows.reshape(-1, batch_rows), live_tokens.reshape(-1, batch_rows)))
    partial_value = partial_value.reshape(owner_ranks, per_rank, QUERY_HEADS, HEAD_SIZE)
    peak_score = peak_score.reshape(owner_ranks, per_rank, QUERY_HEADS)
    weight_sum = weight_sum.reshape(owner_ranks, per_rank, QUERY_HEADS)
    query_head_rows = query_tile_block.reshape(owner_ranks, RANK_REQUESTS, KEY_VALUE_HEADS, heads_per_group, HEAD_SIZE).astype(jnp.float32)
    key_head_rows = fresh_key.reshape(owner_ranks, RANK_REQUESTS, KEY_VALUE_HEADS, HEAD_SIZE).astype(jnp.float32)
    own_score = jnp.einsum("orkgd,orkd->orkg", query_head_rows, key_head_rows, precision=lax.Precision.HIGHEST).reshape(owner_ranks, RANK_REQUESTS, QUERY_HEADS) * score_scale
    member = jnp.transpose(chosen, (0, 2, 1))[..., None]
    ceiling = jnp.maximum(own_score, jnp.max(jnp.where(member, peak_score[:, None], -1e30), axis=2))
    block_weight = jnp.where(member, jnp.exp(peak_score[:, None] - ceiling[:, :, None]) * weight_sum[:, None], 0.0)
    self_weight = jnp.exp(own_score - ceiling)
    value_head_rows = jnp.repeat(fresh_value.reshape(owner_ranks, RANK_REQUESTS, KEY_VALUE_HEADS, HEAD_SIZE), heads_per_group, axis=2).astype(jnp.float32)
    numerator = jnp.einsum("orbh,obhd->orhd", block_weight, partial_value.astype(jnp.float32), precision=lax.Precision.HIGHEST) + self_weight[..., None] * value_head_rows
    denominator = jnp.sum(block_weight, axis=2) + self_weight
    return (numerator / denominator[..., None]).astype(jnp.bfloat16).reshape(request_count, feature_width)


def reference(queries, new_token_keys, new_token_values, key_pool, value_pool, block_list, context_len):
    outputs = [micro_batch(queries[index], new_token_keys[index], new_token_values[index], key_pool, value_pool, block_list[index], context_len[index]) for index in range(queries.shape[0])]
    return jnp.stack(outputs)
```

```python
import functools

import jax
import jax.numpy as jnp
from jax import lax
from jax.experimental import pallas as pl
from jax.experimental.pallas import tpu as pltpu
from jax.sharding import Mesh, PartitionSpec as P

LANES = 128
META = 8
EMPTY = -1e30
PARTS = 3
F32, BF16 = jnp.float32, jnp.bfloat16


def lane_ids(shape):
    return lax.broadcasted_iota(jnp.int32, shape, len(shape) - 1)


def split3(x):
    high = x.astype(BF16).astype(F32)
    rest = x - high
    middle = rest.astype(BF16).astype(F32)
    return high, middle, rest - middle


def joined(tile):
    axis = tile.ndim - 1
    return tile + pltpu.roll(tile, LANES - 1, axis) + pltpu.roll(tile, LANES - 2, axis)


def holder_kernel(
    heads, scale, me, own_ref, sib_ref, key_ref, value_ref, mine_ref, theirs_ref,
    asked, keys, values, parts, table, found, spots, sems, spot_sem,
):
    ranks, rows, _ = asked.shape
    half = ranks // 2
    slots, block_len, _ = keys.shape
    entries = slots
    per_micro = entries // 2
    loads = [
        pltpu.make_async_copy(own_ref, asked.at[pl.ds(0, half)], sems.at[0]),
        pltpu.make_async_copy(sib_ref, asked.at[pl.ds(half, half)], sems.at[1]),
        pltpu.make_async_copy(key_ref, keys, sems.at[2]),
        pltpu.make_async_copy(value_ref, values, sems.at[3]),
    ]
    for load in loads:
        load.start()
    parts[:, : 2 * heads, :] = jnp.zeros((ranks, 2 * heads, LANES), BF16)
    parts[:, 2 * heads :, :] = jnp.full((ranks, META, LANES), EMPTY, BF16)
    loads[0].wait()
    loads[1].wait()
    table[...] = asked[:, 2 * heads :, :].astype(F32).reshape(ranks * META, LANES)
    listed = table[pl.ds(0, ranks, stride=META), :]
    tails = table[pl.ds(1, ranks, stride=META), :]
    lane = lane_ids((ranks, LANES))
    here = (listed == me[0].astype(F32)) & (lane < entries)
    slot = pltpu.roll(listed, LANES // 2, 1)
    code = slot * entries + lane.astype(F32)
    first = jnp.min(jnp.where(here, code, 1e6), axis=1, keepdims=True)
    last = jnp.max(jnp.where(here, code, -1.0), axis=1, keepdims=True)
    valid = last >= 0.0
    row = lax.broadcasted_iota(jnp.int32, (ranks, ranks), 0)
    column = lax.broadcasted_iota(jnp.int32, (ranks, ranks), 1)
    before = jnp.dot(
        (column < row).astype(F32).astype(BF16),
        jnp.broadcast_to(valid.astype(F32), (ranks, LANES)).astype(BF16),
        preferred_element_type=F32,
    )
    chosen = valid & (before == lane.astype(F32))
    rank = lax.broadcasted_iota(jnp.int32, (ranks, LANES), 0).astype(F32)
    tail0 = jnp.sum(jnp.where(lane == 0, tails, 0.0), axis=1, keepdims=True)
    tail1 = jnp.sum(jnp.where(lane == 1, tails, 0.0), axis=1, keepdims=True)

    def listing(x):
        return jnp.sum(jnp.where(chosen, x, 0.0), axis=0, keepdims=True)

    lines = [listing(x) for x in (rank, first, last, tail0, tail1)]
    lines.append(jnp.zeros((8 - len(lines), LANES), F32))
    found[...] = jnp.concatenate(lines, axis=0).astype(jnp.int32)
    move = pltpu.make_async_copy(found, spots, spot_sem)
    move.start()
    move.wait()
    loads[2].wait()
    loads[3].wait()

    pairs = slots // 2
    together = min(4, pairs)
    token = lane_ids((heads, block_len))
    lane8 = lane_ids((8, LANES))

    def step(i, carry):
        work = []
        for k in range(together):
            n = i * together + k
            where = spots[0, n]
            for line in (1, 2):
                block = spots[line, n]
                place = block // entries
                at = block % entries
                micro = at // per_micro
                tail = jnp.where(micro == 0, spots[3, n], spots[4, n])
                live = jnp.where(at % per_micro == per_micro - 1, tail, block_len)
                work.append((where, place, micro, live))
        scores = []
        for where, place, micro, live in work:
            query = asked[where, pl.ds(pl.multiple_of(micro * heads, heads), heads), :]
            score = lax.dot_general(
                query, keys[place], (((1,), (1,)), ((), ())), preferred_element_type=F32
            )
            scores.append(jnp.where(token < live, score * scale, EMPTY))
        score = jnp.concatenate(scores, axis=0)
        peak = jnp.max(score, axis=1, keepdims=True)
        weight = jnp.exp(score - peak)
        total = jnp.sum(weight, axis=1, keepdims=True)
        weight = weight.astype(BF16)
        share = 1.0 / total
        level = peak + jnp.log(total)
        outs = []
        for k, (where, place, micro, live) in enumerate(work):
            mixed = jnp.dot(
                weight[k * heads : (k + 1) * heads], values[place], preferred_element_type=F32
            )
            outs.append(mixed * share[k * heads : (k + 1) * heads])
        for k in range(together):
            where, _, micro_a, _ = work[2 * k]
            _, _, micro_b, _ = work[2 * k + 1]
            level_a = level[2 * k * heads : (2 * k + 1) * heads]
            level_b = level[(2 * k + 1) * heads : (2 * k + 2) * heads]
            tile = jnp.zeros((8, LANES), F32)
            for micro in range(2):
                in_a = (micro_a == micro).astype(F32)
                in_b = (micro_b == micro).astype(F32)
                la = jnp.where(micro_a == micro, level_a, EMPTY)
                lb = jnp.where(micro_b == micro, level_b, EMPTY)
                top = jnp.maximum(la, lb)
                wa = jnp.exp(la - top) * in_a
                wb = jnp.exp(lb - top) * in_b
                both = jnp.maximum(wa + wb, 1e-30)
                part = (outs[2 * k] * wa + outs[2 * k + 1] * wb) / both
                parts[where, micro * heads : (micro + 1) * heads, :] = part.astype(BF16)
                depth = top + jnp.maximum(jnp.log(both), -80.0)
                for piece in range(heads // 8):
                    group = micro * (heads // 8) + piece
                    for j, term in enumerate(split3(depth[piece * 8 : (piece + 1) * 8])):
                        tile = jnp.where(lane8 == PARTS * group + j, term, tile)
            parts[where, 2 * heads :, :] = tile.astype(BF16)
        return carry

    lax.fori_loop(0, pairs // together, step, 0)
    stores = [
        pltpu.make_async_copy(parts.at[pl.ds(half, half)], theirs_ref, sems.at[0]),
        pltpu.make_async_copy(parts.at[pl.ds(0, half)], mine_ref, sems.at[1]),
    ]
    for store in stores:
        store.start()
    for store in stores:
        store.wait()


def merge_kernel(heads, chunk, a_ref, b_ref, out_ref):
    count = a_ref.shape[0]
    groups = 2 * heads // 8
    lane = lane_ids((chunk, 8, LANES))

    def step(i, carry):
        at = pl.ds(i * chunk, chunk)
        la = joined(a_ref[at, 2 * heads :, :].astype(F32))
        lb = joined(b_ref[at, 2 * heads :, :].astype(F32))
        top = jnp.maximum(la, lb)
        wa, wb = jnp.exp(la - top), jnp.exp(lb - top)
        both = wa + wb
        share = wa / both
        depth = top + jnp.log(both)
        depth_tile = jnp.zeros((chunk, 8, LANES), F32)
        terms = split3(depth)
        for j, term in enumerate(terms):
            moved = term if j == 0 else pltpu.roll(term, j, 2)
            depth_tile = jnp.where(lane % PARTS == j, moved, depth_tile)
        out_ref[at, 2 * heads :, :] = jnp.where(
            lane < PARTS * groups, depth_tile, 0.0
        ).astype(BF16)
        a = a_ref[at, : 2 * heads, :].astype(F32)
        b = b_ref[at, : 2 * heads, :].astype(F32)
        scale = jnp.concatenate(
            [
                jnp.broadcast_to(
                    share[:, :, PARTS * g : PARTS * g + 1], (chunk, 8, LANES)
                )
                for g in range(groups)
            ],
            axis=1,
        )
        out_ref[at, : 2 * heads, :] = (b + scale * (a - b)).astype(BF16)
        return carry

    lax.fori_loop(0, count // chunk, step, 0)


def owner_kernel(heads, scale, part_ref, query_ref, key_ref, value_ref, out_ref):
    count = part_ref.shape[0]
    pieces = heads // 8
    groups = 2 * pieces
    lane = lane_ids((8, LANES))
    query = query_ref[...].astype(F32)
    own = jnp.zeros((8, LANES), F32)
    for g in range(groups):
        micro = g // pieces
        key = key_ref[micro : micro + 1, :].astype(F32)
        score = jnp.sum(query[g * 8 : (g + 1) * 8] * key, axis=1, keepdims=True) * scale
        own = jnp.where(lane == PARTS * g, score, own)
    level = joined(part_ref[:, 2 * heads :, :].astype(F32))
    top = jnp.maximum(jnp.max(level, axis=0), own)
    weight = jnp.exp(level - top[None])
    self_weight = jnp.exp(own - top)
    total = jnp.sum(weight, axis=0) + self_weight
    for g in range(groups):
        micro, piece = g // pieces, g % pieces
        if piece == 0:
            rows = part_ref[:, micro * heads : (micro + 1) * heads, :].astype(F32)
        at = PARTS * g
        column = jnp.broadcast_to(weight[:, :, at : at + 1], (count, 8, LANES))
        mixed = jnp.sum(column * rows[:, piece * 8 : (piece + 1) * 8, :], axis=0)
        value = value_ref[micro : micro + 1, :].astype(F32)
        mixed = mixed + self_weight[:, at : at + 1] * value
        out_ref[g * 8 : (g + 1) * 8, :] = mixed / total[:, at : at + 1]


def exchange(x, axis):
    return lax.all_to_all(x, axis, 0, 0)


def per_device(
    queries, new_token_keys, new_token_values, key_pool, value_pool, block_list, context_len
):
    planes, tensor = lax.axis_size("zy"), lax.axis_size("tp")
    micros, _, width = queries.shape
    slots, block_len, dim = key_pool.shape
    heads = width // dim
    scale = dim ** (-0.5)
    rows = micros * heads + META
    swap = [(0, 1), (1, 0)]
    any_space = pl.BlockSpec(memory_space=pl.ANY)
    vmem = pl.BlockSpec(memory_space=pltpu.VMEM)
    params = pltpu.CompilerParams(vmem_limit_bytes=40 * 1024 * 1024)
    message = jax.ShapeDtypeStruct((planes, rows, LANES), BF16)

    with jax.named_scope("entries_over_tp"):
        quarter = block_list.reshape(1, 1, -1).astype(BF16)
        size = quarter.shape[-1]
        quarter = jnp.pad(quarter, ((0, 0), (0, 7), (0, LANES - size)))
        quarters = exchange(jnp.broadcast_to(quarter, (tensor, 8, LANES)), "tp")
        listed = quarters[:, 0, :size].reshape(tensor, micros, -1, 2)
        listed = listed.transpose(3, 1, 0, 2).reshape(2, slots)
        listed = jnp.pad(listed, ((0, 0), (0, LANES // 2 - slots))).reshape(1, LANES)
    with jax.named_scope("queries_to_holders"):
        query = queries.reshape(micros * heads, dim)
        tail = context_len.reshape(1, micros) - (slots // micros - 1) * block_len
        tail = jnp.pad(tail.astype(BF16), ((0, META - 2), (0, LANES - micros)))
        packed = jnp.concatenate([query, listed, tail], axis=0)
        own = exchange(jnp.broadcast_to(packed[None], (planes, rows, LANES)), "zy")
        sibling = lax.ppermute(own, "c", swap)
    with jax.named_scope("block_attention"):
        me = (lax.axis_index("zy") * 2 + lax.axis_index("c")).astype(jnp.int32).reshape(1)
        ranks = 2 * planes
        mine, theirs = pl.pallas_call(
            functools.partial(holder_kernel, heads, scale),
            out_shape=(message, message),
            in_specs=[pl.BlockSpec(memory_space=pltpu.SMEM)] + [any_space] * 4,
            out_specs=(any_space, any_space),
            scratch_shapes=[
                pltpu.VMEM((ranks, rows, LANES), BF16),
                pltpu.VMEM(key_pool.shape, BF16),
                pltpu.VMEM(value_pool.shape, BF16),
                pltpu.VMEM((ranks, rows, LANES), BF16),
                pltpu.VMEM((ranks * META, LANES), F32),
                pltpu.VMEM((8, LANES), jnp.int32),
                pltpu.SMEM((8, LANES), jnp.int32),
                pltpu.SemaphoreType.DMA((4,)),
                pltpu.SemaphoreType.DMA,
            ],
            compiler_params=params,
        )(me, own, sibling, key_pool, value_pool)
    with jax.named_scope("parts_to_owners"):
        other = lax.ppermute(theirs, "c", swap)
        merged = pl.pallas_call(
            functools.partial(merge_kernel, heads, min(8, planes)),
            out_shape=message,
            in_specs=[vmem, vmem],
            out_specs=vmem,
            compiler_params=params,
        )(mine, other)
        arrived = exchange(merged, "zy")
    with jax.named_scope("owner_sum"):
        out = pl.pallas_call(
            functools.partial(owner_kernel, heads, scale),
            out_shape=jax.ShapeDtypeStruct((micros * heads, dim), F32),
            in_specs=[vmem] * 4,
            out_specs=vmem,
            compiler_params=params,
        )(arrived, query, new_token_keys.reshape(micros, dim), new_token_values.reshape(micros, dim))
        return out.astype(BF16).reshape(micros, 1, width)


def solution(mesh):
    spread, tensor = mesh.devices.shape
    finer = Mesh(mesh.devices.reshape(spread // 2, 2, tensor), ("zy", "c", "tp"))
    dp = ("zy", "c")
    placed = (
        P(None, dp, "tp"),
        P(None, dp, "tp"),
        P(None, dp, "tp"),
        P(dp, None, "tp"),
        P(dp, None, "tp"),
        P(None, ("zy", "c", "tp"), None),
        P(None, dp),
    )
    return jax.shard_map(
        per_device, mesh=finer, in_specs=placed, out_specs=P(None, dp, "tp"), check_vma=False
    )
```

```python
import functools

import jax
import jax.numpy as jnp
from jax import lax
from jax.experimental import pallas as pl
from jax.experimental.pallas import tpu as pltpu
from jax.sharding import Mesh, PartitionSpec as P

LANES = 128
FIELD = 16
SPAN = 32
EMPTY = -1e30
PARTS = 3
F32, BF16 = jnp.float32, jnp.bfloat16


def lane_ids(shape):
    return lax.broadcasted_iota(jnp.int32, shape, len(shape) - 1)


def split3(x):
    high = x.astype(BF16).astype(F32)
    rest = x - high
    middle = rest.astype(BF16).astype(F32)
    return high, middle, rest - middle


def joined(row):
    return row + pltpu.roll(row, LANES - 1, 1) + pltpu.roll(row, LANES - 2, 1)


def turned(tile, back):
    sublane = lax.broadcasted_iota(jnp.int32, tile.shape, 0)
    for bit in (1, 2, 4):
        shift = bit * FIELD
        moved = pltpu.roll(tile, LANES - shift if back else shift, 1)
        tile = jnp.where((sublane & bit) != 0, moved, tile)
    return tile


def to_row(tile):
    return jnp.sum(turned(tile, False), axis=0, keepdims=True)


def to_tile(row):
    return turned(jnp.broadcast_to(row, (8, LANES)), True)


def column(tile, group):
    at = PARTS * group
    return jnp.broadcast_to(tile[:, at : at + 1], (8, LANES))


def pack_kernel(first_tail, query_ref, list_ref, length_ref, out_ref, wide, rows):
    heads, micros, _ = query_ref.shape
    per = list_ref.shape[2]
    wide[...] = query_ref[...].astype(F32)
    query = jnp.concatenate([wide[:, m, :] for m in range(micros)], axis=0).astype(BF16)
    rows[...] = jnp.zeros(rows.shape, F32)
    for m in range(micros):
        rows[2 * m : 2 * m + 2, :per] = list_ref[m].astype(F32)
    rows[2 * micros : 2 * micros + 1, :micros] = (length_ref[...] - first_tail).astype(F32)
    listed = rows[2 * micros : 2 * micros + 1, :]
    listed = pltpu.roll(listed, 2 * FIELD, 1)
    for m in range(micros):
        for field in range(2):
            at = 2 * m + field
            shift = field * FIELD + m * per
            row = rows[at : at + 1, :]
            listed = listed + (pltpu.roll(row, shift, 1) if shift else row)
    listed = jnp.concatenate([listed, jnp.zeros((1, LANES), F32)], axis=0).astype(BF16)
    message = jnp.concatenate([query.reshape(heads, micros, LANES), listed[None]], axis=0)
    out_ref[...] = jnp.broadcast_to(message[None], out_ref.shape)


def holder_kernel(
    heads, scale, tensor, per, me, own_ref, sib_ref, entry_ref, key_ref, value_ref,
    mine_ref, theirs_ref, keys, values, found, spots, sems, spot_sem,
):
    half = own_ref.shape[0]
    ranks = 2 * half
    slots, block_len, _ = keys.shape
    entries = slots
    per_micro = entries // 2
    loads = [
        pltpu.make_async_copy(key_ref, keys, sems.at[0]),
        pltpu.make_async_copy(value_ref, values, sems.at[1]),
    ]
    for load in loads:
        load.start()

    core = me[0] % 2
    lane = lane_ids((ranks, LANES))
    quarters = []
    for t in range(tensor):
        quarters.append(
            jnp.concatenate(
                [
                    entry_ref[core * tensor + t].astype(F32),
                    entry_ref[(1 - core) * tensor + t].astype(F32),
                ],
                axis=0,
            )
        )
    tails = quarters[0]
    listed = jnp.zeros((ranks, LANES), F32)
    for t, quarter in enumerate(quarters):
        moved = pltpu.roll(quarter, t * SPAN, 1) if t else quarter
        listed = jnp.where(lane // SPAN == t, moved, listed)
    index = lane % FIELD
    order = (index // (per // 2)) * per_micro + (lane // SPAN) * (per // 2) + index % (per // 2)
    here = (listed == me[0].astype(F32)) & (lane % SPAN < per) & (lane < tensor * SPAN)
    slot = pltpu.roll(listed, LANES - FIELD, 1)
    code = slot * entries + order.astype(F32)
    first = jnp.min(jnp.where(here, code, 1e6), axis=1, keepdims=True)
    last = jnp.max(jnp.where(here, code, -1.0), axis=1, keepdims=True)
    valid = last >= 0.0
    row = lax.broadcasted_iota(jnp.int32, (ranks, ranks), 0)
    ahead = lax.broadcasted_iota(jnp.int32, (ranks, ranks), 1)
    before = jnp.dot(
        (ahead < row).astype(F32).astype(BF16),
        jnp.broadcast_to(valid.astype(F32), (ranks, LANES)).astype(BF16),
        preferred_element_type=F32,
    )
    chosen = valid & (before == lane.astype(F32))
    rank = lax.broadcasted_iota(jnp.int32, (ranks, LANES), 0).astype(F32)
    tail0 = jnp.sum(jnp.where(lane == 2 * FIELD, tails, 0.0), axis=1, keepdims=True)
    tail1 = jnp.sum(jnp.where(lane == 2 * FIELD + 1, tails, 0.0), axis=1, keepdims=True)

    def listing(x):
        return jnp.sum(jnp.where(chosen, x, 0.0), axis=0, keepdims=True)

    lines = [listing(x) for x in (rank, first, last, tail0, tail1)]
    lines.append(jnp.zeros((8 - len(lines), LANES), F32))
    found[...] = jnp.concatenate(lines, axis=0).astype(jnp.int32)
    move = pltpu.make_async_copy(found, spots, spot_sem)
    move.start()
    for ref in (mine_ref, theirs_ref):
        ref[:, :heads] = jnp.zeros((half, heads, 2, LANES), BF16)
        ref[:, heads] = jnp.full((half, 2, LANES), EMPTY, BF16)
    move.wait()
    for load in loads:
        load.wait()

    pairs = slots // 2
    together = min(4, pairs)
    token = lane_ids((heads, block_len))
    lane8 = lane_ids((8, LANES))

    def step(i, carry):
        work = []
        for k in range(together):
            n = i * together + k
            where = spots[0, n]
            for line in (1, 2):
                block = spots[line, n]
                place = block // entries
                at = block % entries
                micro = at // per_micro
                tail = jnp.where(micro == 0, spots[3, n], spots[4, n])
                live = jnp.where(at % per_micro == per_micro - 1, tail, block_len)
                work.append((where, place, micro, live))
        scores = []
        for where, place, micro, live in work:
            inner = pl.ds(micro * (heads // 2), heads // 2)
            query = jnp.where(
                where < half, own_ref[where % half, inner], sib_ref[where % half, inner]
            ).reshape(heads, LANES)
            score = lax.dot_general(
                query, keys[place], (((1,), (1,)), ((), ())), preferred_element_type=F32
            )
            scores.append(jnp.where(token < live, score * scale, EMPTY))
        score = jnp.concatenate(scores, axis=0)
        peak = jnp.max(score, axis=1, keepdims=True)
        weight = jnp.exp(score - peak)
        total = jnp.sum(weight, axis=1, keepdims=True)
        weight = weight.astype(BF16)
        share = 1.0 / total
        level = peak + jnp.log(total)
        outs = []
        for k, (where, place, micro, live) in enumerate(work):
            mixed = jnp.dot(
                weight[k * heads : (k + 1) * heads], values[place], preferred_element_type=F32
            )
            outs.append(mixed * share[k * heads : (k + 1) * heads])
        for k in range(together):
            where, _, micro_a, _ = work[2 * k]
            _, _, micro_b, _ = work[2 * k + 1]
            level_a = level[2 * k * heads : (2 * k + 1) * heads]
            level_b = level[(2 * k + 1) * heads : (2 * k + 2) * heads]
            tile = jnp.zeros((8, LANES), F32)
            rows = []
            for micro in range(2):
                in_a = (micro_a == micro).astype(F32)
                in_b = (micro_b == micro).astype(F32)
                la = jnp.where(micro_a == micro, level_a, EMPTY)
                lb = jnp.where(micro_b == micro, level_b, EMPTY)
                top = jnp.maximum(la, lb)
                wa = jnp.exp(la - top) * in_a
                wb = jnp.exp(lb - top) * in_b
                both = jnp.maximum(wa + wb, 1e-30)
                part = (outs[2 * k] * wa + outs[2 * k + 1] * wb) / both
                rows.append(part)
                depth = top + jnp.maximum(jnp.log(both), -80.0)
                for piece in range(heads // 8):
                    group = micro * (heads // 8) + piece
                    for j, term in enumerate(split3(depth[piece * 8 : (piece + 1) * 8])):
                        tile = jnp.where(lane8 == PARTS * group + j, term, tile)
            depths = jnp.concatenate([to_row(tile), jnp.zeros((1, LANES), F32)], axis=0)
            part = jnp.concatenate(rows, axis=0).astype(BF16).reshape(heads, 2, LANES)
            for ref, chosen_here in ((mine_ref, where < half), (theirs_ref, where >= half)):

                @pl.when(chosen_here)
                def _():
                    ref[where % half, :heads] = part
                    ref[where % half, heads] = depths.astype(BF16)

        return carry

    lax.fori_loop(0, pairs // together, step, 0)


def merge_kernel(heads, a_ref, b_ref, out_ref, shares):
    count = a_ref.shape[0]
    groups = 2 * heads // 8
    lane = lane_ids((2 * count, LANES)) % FIELD
    la = joined(a_ref[:, heads].astype(F32).reshape(2 * count, LANES))
    lb = joined(b_ref[:, heads].astype(F32).reshape(2 * count, LANES))
    top = jnp.maximum(la, lb)
    wa, wb = jnp.exp(la - top), jnp.exp(lb - top)
    both = wa + wb
    shares[...] = wa / both
    depth = top + jnp.log(both)
    row = jnp.zeros(depth.shape, F32)
    for j, term in enumerate(split3(depth)):
        moved = pltpu.roll(term, j, 1) if j else term
        row = jnp.where((lane % PARTS == j) & (lane < PARTS * groups), moved, row)
    out_ref[:, heads] = row.astype(BF16).reshape(count, 2, LANES)

    def step(e, carry):
        tile = to_tile(shares[pl.ds(2 * e, 1), :])
        scale = jnp.concatenate([column(tile, g) for g in range(groups)], axis=0)
        a = a_ref[e, :heads].reshape(2 * heads, LANES).astype(F32)
        b = b_ref[e, :heads].reshape(2 * heads, LANES).astype(F32)
        out_ref[e, :heads] = (b + scale * (a - b)).astype(BF16).reshape(heads, 2, LANES)
        return carry

    lax.fori_loop(0, count, step, 0, unroll=min(8, count))


def owner_kernel(heads, scale, part_ref, query_ref, key_ref, value_ref, out_ref, weights, wide):
    count = part_ref.shape[0]
    pieces = heads // 8
    groups = 2 * pieces
    lane = lane_ids((8, LANES))
    wide[...] = query_ref[...].astype(F32)
    own = jnp.zeros((8, LANES), F32)
    for g in range(groups):
        micro, piece = g // pieces, g % pieces
        query = wide[piece * 8 : (piece + 1) * 8, micro, :]
        key = key_ref[micro : micro + 1, :].astype(F32)
        score = jnp.sum(query * key, axis=1, keepdims=True) * scale
        own = jnp.where(lane == PARTS * g, score, own)
    own = to_row(own)
    level = joined(part_ref[:, heads].astype(F32).reshape(2 * count, LANES))
    line = lax.broadcasted_iota(jnp.int32, level.shape, 0)
    level = jnp.where(line % 2 == 0, level, EMPTY)
    top = jnp.maximum(jnp.max(level, axis=0, keepdims=True), own)
    weight = jnp.exp(level - top)
    weights[...] = weight
    self_weight = jnp.exp(own - top)
    total = to_tile(jnp.sum(weight, axis=0, keepdims=True) + self_weight)
    self_weight = to_tile(self_weight)

    def step(e, mixed):
        tile = to_tile(weights[pl.ds(2 * e, 1), :])
        scale = jnp.concatenate([column(tile, g) for g in range(groups)], axis=0)
        return mixed + scale * part_ref[e, :heads].reshape(2 * heads, LANES).astype(F32)

    mixed = lax.fori_loop(
        0, count, step, jnp.zeros((2 * heads, LANES), F32), unroll=min(8, count)
    )
    for g in range(groups):
        micro, piece = g // pieces, g % pieces
        value = value_ref[micro : micro + 1, :].astype(F32)
        part = mixed[g * 8 : (g + 1) * 8] + column(self_weight, g) * value
        wide[piece * 8 : (piece + 1) * 8, micro, :] = part / column(total, g)
    out_ref[...] = wide[...].astype(BF16)


def exchange(x, axis):
    return lax.all_to_all(x, axis, 0, 0)


def per_device(
    queries, new_token_keys, new_token_values, key_pool, value_pool, block_list, context_len
):
    planes, tensor = lax.axis_size("zy"), lax.axis_size("tp")
    micros, _, width = queries.shape
    slots, block_len, dim = key_pool.shape
    heads = width // dim
    scale = dim ** (-0.5)
    per = slots // tensor
    swap = [(0, 1), (1, 0)]
    hbm = pl.BlockSpec(memory_space=pltpu.HBM)
    vmem = pl.BlockSpec(memory_space=pltpu.VMEM)
    params = pltpu.CompilerParams(vmem_limit_bytes=32 * 1024 * 1024)
    message = jax.ShapeDtypeStruct((planes, heads + 1, micros, LANES), BF16)
    query = queries.reshape(micros, heads, dim).transpose(1, 0, 2)

    with jax.named_scope("queries_to_holders"):
        packed = pl.pallas_call(
            functools.partial(pack_kernel, (slots // micros - 1) * block_len),
            out_shape=message,
            in_specs=[vmem] * 3,
            out_specs=vmem,
            scratch_shapes=[pltpu.VMEM(query.shape, F32), pltpu.VMEM((8, LANES), F32)],
            compiler_params=params,
        )(query, block_list.transpose(0, 2, 1), context_len.transpose(1, 0))
        own = exchange(packed, "zy")
        sibling = lax.ppermute(own, "c", swap)
        rows = own[:, heads, 0]
        rows = exchange(
            jnp.broadcast_to(rows[None], (2 * tensor, planes, LANES)), ("c", "tp")
        )
    with jax.named_scope("block_attention"):
        me = (lax.axis_index("zy") * 2 + lax.axis_index("c")).astype(jnp.int32).reshape(1)
        mine, theirs = pl.pallas_call(
            functools.partial(holder_kernel, heads, scale, tensor, per),
            out_shape=(message, message),
            in_specs=[pl.BlockSpec(memory_space=pltpu.SMEM)] + [vmem] * 3 + [hbm] * 2,
            out_specs=(vmem, vmem),
            scratch_shapes=[
                pltpu.VMEM(key_pool.shape, BF16),
                pltpu.VMEM(value_pool.shape, BF16),
                pltpu.VMEM((8, LANES), jnp.int32),
                pltpu.SMEM((8, LANES), jnp.int32),
                pltpu.SemaphoreType.DMA((2,)),
                pltpu.SemaphoreType.DMA,
            ],
            compiler_params=params,
        )(me, own, sibling, rows, key_pool, value_pool)
    with jax.named_scope("parts_to_owners"):
        other = lax.ppermute(theirs, "c", swap)
        merged = pl.pallas_call(
            functools.partial(merge_kernel, heads),
            out_shape=message,
            in_specs=[vmem, vmem],
            out_specs=vmem,
            scratch_shapes=[pltpu.VMEM((2 * planes, LANES), F32)],
            compiler_params=params,
        )(mine, other)
        arrived = exchange(merged, "zy")
    with jax.named_scope("owner_sum"):
        out = pl.pallas_call(
            functools.partial(owner_kernel, heads, scale),
            out_shape=jax.ShapeDtypeStruct(query.shape, BF16),
            in_specs=[vmem] * 4,
            out_specs=vmem,
            scratch_shapes=[
                pltpu.VMEM((2 * planes, LANES), F32),
                pltpu.VMEM(query.shape, F32),
            ],
            compiler_params=params,
        )(arrived, query, new_token_keys.reshape(micros, dim), new_token_values.reshape(micros, dim))
        return out.transpose(1, 0, 2).reshape(micros, 1, width)


def solution(mesh):
    spread, tensor = mesh.devices.shape
    finer = Mesh(mesh.devices.reshape(spread // 2, 2, tensor), ("zy", "c", "tp"))
    dp = ("zy", "c")
    placed = (
        P(None, dp, "tp"),
        P(None, dp, "tp"),
        P(None, dp, "tp"),
        P(dp, None, "tp"),
        P(dp, None, "tp"),
        P(None, ("zy", "c", "tp"), None),
        P(None, dp),
    )
    return jax.shard_map(
        per_device, mesh=finer, in_specs=placed, out_specs=P(None, dp, "tp"), check_vma=False
    )
```

```python
import functools

import jax
import jax.numpy as jnp
from jax import lax
from jax.experimental import pallas as pl
from jax.experimental.pallas import tpu as pltpu
from jax.sharding import Mesh, PartitionSpec as P

LANES = 128
FIELD = 16
SPAN = 32
EMPTY = -1e30
PARTS = 3
F32, BF16 = jnp.float32, jnp.bfloat16


def lane_ids(shape):
    return lax.broadcasted_iota(jnp.int32, shape, len(shape) - 1)


def split3(x):
    high = x.astype(BF16).astype(F32)
    rest = x - high
    middle = rest.astype(BF16).astype(F32)
    return high, middle, rest - middle


def joined(row):
    return row + pltpu.roll(row, LANES - 1, 1) + pltpu.roll(row, LANES - 2, 1)


def spread_levels(rows, groups):
    count = rows.shape[0] // 2
    line = lax.broadcasted_iota(jnp.int32, (8 * count, 2 * count), 0)
    source = lax.broadcasted_iota(jnp.int32, (8 * count, 2 * count), 1)
    pick = (source == (line // 8) * 2).astype(F32).astype(BF16)
    copies = jnp.dot(pick, rows, preferred_element_type=F32)
    sublane = lax.broadcasted_iota(jnp.int32, copies.shape, 0) % 8
    copies = jnp.where(lane_ids(copies.shape) // FIELD == sublane, copies, 0.0).astype(BF16)
    at = lax.broadcasted_iota(jnp.int32, (LANES, groups * LANES), 0) % FIELD // PARTS
    group = lane_ids((LANES, groups * LANES)) // LANES
    add = (at == group).astype(F32).astype(BF16)
    levels = jnp.dot(copies, add, preferred_element_type=F32)
    return [levels[:, g * LANES : (g + 1) * LANES] for g in range(groups)]


def pack_kernel(per, query_ref, list_ref, out_ref, wide):
    heads, micros, _ = query_ref.shape
    wide[...] = query_ref[...].astype(F32)
    query = jnp.concatenate([wide[:, m, :] for m in range(micros)], axis=0).astype(BF16)
    row = pltpu.roll(list_ref[micros].astype(F32)[:1], 2 * FIELD, 1)
    for m in range(micros):
        fields = list_ref[m].astype(F32)
        for field in range(2):
            shift = field * FIELD + m * per
            entry = fields[field : field + 1]
            row = row + (pltpu.roll(entry, shift, 1) if shift else entry)
    listed = jnp.concatenate([row, jnp.zeros((1, LANES), F32)], axis=0).astype(BF16)
    message = jnp.concatenate([query.reshape(heads, micros, LANES), listed[None]], axis=0)
    out_ref[...] = jnp.broadcast_to(message[None], out_ref.shape)


def holder_kernel(
    heads, scale, tensor, per, me, own_ref, sib_ref, entry_ref, key_ref, value_ref,
    mine_ref, theirs_ref, keys, values, parts, tiles, pad, found, spots, sems, spot_sem,
):
    half = own_ref.shape[0]
    ranks = 2 * half
    slots, block_len, _ = keys.shape
    entries = slots
    per_micro = entries // 2
    groups = 2 * heads // 8
    loads = [
        pltpu.make_async_copy(key_ref, keys, sems.at[0]),
        pltpu.make_async_copy(value_ref, values, sems.at[1]),
    ]
    for load in loads:
        load.start()

    core = me[0] % 2
    lane = lane_ids((ranks, LANES))
    quarters = []
    for t in range(tensor):
        quarters.append(
            jnp.concatenate(
                [
                    entry_ref[core * tensor + t].astype(F32),
                    entry_ref[(1 - core) * tensor + t].astype(F32),
                ],
                axis=0,
            )
        )
    tails = quarters[0]
    listed = jnp.zeros((ranks, LANES), F32)
    for t, quarter in enumerate(quarters):
        moved = pltpu.roll(quarter, t * SPAN, 1) if t else quarter
        listed = jnp.where(lane // SPAN == t, moved, listed)
    index = lane % FIELD
    order = (index // (per // 2)) * per_micro + (lane // SPAN) * (per // 2) + index % (per // 2)
    here = (listed == me[0].astype(F32)) & (lane % SPAN < per) & (lane < tensor * SPAN)
    slot = pltpu.roll(listed, LANES - FIELD, 1)
    code = slot * entries + order.astype(F32)
    first = jnp.min(jnp.where(here, code, 1e6), axis=1, keepdims=True)
    last = jnp.max(jnp.where(here, code, -1.0), axis=1, keepdims=True)
    valid = last >= 0.0
    row = lax.broadcasted_iota(jnp.int32, (ranks, ranks), 0)
    ahead = lax.broadcasted_iota(jnp.int32, (ranks, ranks), 1)
    before = jnp.dot(
        (ahead < row).astype(F32).astype(BF16),
        jnp.broadcast_to(valid.astype(F32), (ranks, LANES)).astype(BF16),
        preferred_element_type=F32,
    )
    chosen = valid & (before == lane.astype(F32))
    rank = lax.broadcasted_iota(jnp.int32, (ranks, LANES), 0).astype(F32)
    tail0 = jnp.sum(jnp.where(lane == 2 * FIELD, tails, 0.0), axis=1, keepdims=True)
    tail1 = jnp.sum(jnp.where(lane == 2 * FIELD + 1, tails, 0.0), axis=1, keepdims=True)

    def listing(x):
        return jnp.sum(jnp.where(chosen, x, 0.0), axis=0, keepdims=True)

    lines = [listing(x) for x in (rank, first, last, tail0, tail1)]
    lines.append(jnp.zeros((8 - len(lines), LANES), F32))
    found[...] = jnp.concatenate(lines, axis=0).astype(jnp.int32)
    move = pltpu.make_async_copy(found, spots, spot_sem)
    move.start()
    parts[:, :heads] = jnp.zeros((ranks, heads, 2, LANES), BF16)
    ours = lane_ids((8, LANES)) // FIELD == lax.broadcasted_iota(jnp.int32, (8, LANES), 0)
    field = jnp.where(ours, lane_ids((8, LANES)) % FIELD, FIELD)
    blank = jnp.where(field < PARTS * groups, EMPTY, 0.0)
    tiles[...] = jnp.broadcast_to(blank[None], (ranks, 8, LANES)).reshape(ranks * 8, LANES)
    pad[...] = jnp.zeros(pad.shape, F32)
    move.wait()
    for load in loads:
        load.wait()

    pairs = slots // 2
    together = min(4, pairs)
    token = lane_ids((heads, block_len))

    def step(i, carry):
        work = []
        for k in range(together):
            n = i * together + k
            where = spots[0, n]
            for line in (1, 2):
                block = spots[line, n]
                place = block // entries
                at = block % entries
                micro = at // per_micro
                tail = jnp.where(micro == 0, spots[3, n], spots[4, n])
                live = jnp.where(at % per_micro == per_micro - 1, tail, block_len)
                work.append((where, place, micro, live))
        scores = []
        for where, place, micro, live in work:
            inner = pl.ds(micro * (heads // 2), heads // 2)
            query = jnp.where(
                where < half, own_ref[where % half, inner], sib_ref[where % half, inner]
            ).reshape(heads, LANES)
            score = lax.dot_general(
                query, keys[place], (((1,), (1,)), ((), ())), preferred_element_type=F32
            )
            scores.append(jnp.where(token < live, score * scale, EMPTY))
        score = jnp.concatenate(scores, axis=0)
        peak = jnp.max(score, axis=1, keepdims=True)
        weight = jnp.exp(score - peak)
        total = jnp.sum(weight, axis=1, keepdims=True)
        weight = weight.astype(BF16)
        share = 1.0 / total
        level = peak + jnp.log(total)
        outs = []
        for k, (where, place, micro, live) in enumerate(work):
            mixed = jnp.dot(
                weight[k * heads : (k + 1) * heads], values[place], preferred_element_type=F32
            )
            outs.append(mixed * share[k * heads : (k + 1) * heads])
        for k in range(together):
            where, _, micro_a, _ = work[2 * k]
            _, _, micro_b, _ = work[2 * k + 1]
            level_a = level[2 * k * heads : (2 * k + 1) * heads]
            level_b = level[(2 * k + 1) * heads : (2 * k + 2) * heads]
            tile = jnp.zeros((8, LANES), F32)
            rows = []
            for micro in range(2):
                in_a = (micro_a == micro).astype(F32)
                in_b = (micro_b == micro).astype(F32)
                la = jnp.where(micro_a == micro, level_a, EMPTY)
                lb = jnp.where(micro_b == micro, level_b, EMPTY)
                top = jnp.maximum(la, lb)
                wa = jnp.exp(la - top) * in_a
                wb = jnp.exp(lb - top) * in_b
                both = jnp.maximum(wa + wb, 1e-30)
                rows.append((outs[2 * k] * wa + outs[2 * k + 1] * wb) / both)
                depth = top + jnp.maximum(jnp.log(both), -80.0)
                for piece in range(heads // 8):
                    group = micro * (heads // 8) + piece
                    for j, term in enumerate(split3(depth[piece * 8 : (piece + 1) * 8])):
                        tile = jnp.where(field == PARTS * group + j, term, tile)
            tiles[pl.ds(pl.multiple_of(where * 8, 8), 8), :] = tile
            part = jnp.concatenate(rows, axis=0).astype(BF16).reshape(heads, 2, LANES)
            parts[where, :heads] = part
        return carry

    lax.fori_loop(0, pairs // together, step, 0)
    pad[:, 0, :] = jnp.sum(tiles[...].reshape(ranks, 8, LANES), axis=1)
    parts[:, heads] = pad[...].astype(BF16)
    stores = [
        pltpu.make_async_copy(parts.at[pl.ds(half, half)], theirs_ref, sems.at[0]),
        pltpu.make_async_copy(parts.at[pl.ds(0, half)], mine_ref, sems.at[1]),
    ]
    for store in stores:
        store.start()
    for store in stores:
        store.wait()


def merge_kernel(heads, a_ref, b_ref, out_ref):
    count = a_ref.shape[0]
    groups = 2 * heads // 8
    lane = lane_ids((2 * count, LANES)) % FIELD
    rows_a = a_ref[:, heads].reshape(2 * count, LANES)
    rows_b = b_ref[:, heads].reshape(2 * count, LANES)
    la, lb = joined(rows_a.astype(F32)), joined(rows_b.astype(F32))
    top = jnp.maximum(la, lb)
    depth = top + jnp.log(jnp.exp(la - top) + jnp.exp(lb - top))
    row = jnp.zeros(depth.shape, F32)
    for j, term in enumerate(split3(depth)):
        moved = pltpu.roll(term, j, 1) if j else term
        row = jnp.where((lane % PARTS == j) & (lane < PARTS * groups), moved, row)
    out_ref[:, heads] = row.astype(BF16).reshape(count, 2, LANES)
    spread_a = spread_levels(rows_a, groups)
    spread_b = spread_levels(rows_b, groups)
    for g in range(groups):
        share = 1.0 / (1.0 + jnp.exp(spread_b[g] - spread_a[g]))
        at = slice(4 * g, 4 * (g + 1))
        a = a_ref[:, at].reshape(8 * count, LANES).astype(F32)
        b = b_ref[:, at].reshape(8 * count, LANES).astype(F32)
        merged = (b + share * (a - b)).astype(BF16)
        out_ref[:, at] = merged.reshape(count, 4, 2, LANES)


def owner_kernel(heads, scale, part_ref, query_ref, key_ref, value_ref, out_ref, wide):
    count = part_ref.shape[0]
    pieces = heads // 8
    groups = 2 * pieces
    wide[...] = query_ref[...].astype(F32)
    levels = spread_levels(part_ref[:, heads].reshape(2 * count, LANES), groups)
    for g in range(groups):
        micro, piece = g // pieces, g % pieces
        rows = slice(piece * 8, (piece + 1) * 8)
        key = key_ref[micro : micro + 1, :].astype(F32)
        own = jnp.sum(wide[rows, micro, :] * key, axis=1, keepdims=True) * scale
        level = levels[g].reshape(count, 8, LANES)
        top = jnp.maximum(jnp.max(level, axis=0), own)
        weight = jnp.exp(level - top[None])
        self_weight = jnp.exp(own - top)
        part = part_ref[:, 4 * g : 4 * (g + 1)].reshape(8 * count, LANES).astype(F32)
        mixed = jnp.sum(weight * part.reshape(count, 8, LANES), axis=0)
        mixed = mixed + self_weight * value_ref[micro : micro + 1, :].astype(F32)
        wide[rows, micro, :] = mixed / (jnp.sum(weight, axis=0) + self_weight)
    out_ref[...] = wide[...].astype(BF16)


def exchange(x, axis):
    return lax.all_to_all(x, axis, 0, 0)


def per_device(
    queries, new_token_keys, new_token_values, key_pool, value_pool, block_list, context_len
):
    planes, tensor = lax.axis_size("zy"), lax.axis_size("tp")
    micros, _, width = queries.shape
    slots, block_len, dim = key_pool.shape
    heads = width // dim
    scale = dim ** (-0.5)
    per = slots // tensor
    swap = [(0, 1), (1, 0)]
    hbm = pl.BlockSpec(memory_space=pltpu.HBM)
    vmem = pl.BlockSpec(memory_space=pltpu.VMEM)
    params = pltpu.CompilerParams(vmem_limit_bytes=32 * 1024 * 1024)
    large = pltpu.CompilerParams(vmem_limit_bytes=50 * 1024 * 1024)
    message = jax.ShapeDtypeStruct((planes, heads + 1, micros, LANES), BF16)
    query = queries.reshape(micros, heads, dim).transpose(1, 0, 2)

    with jax.named_scope("queries_to_holders"):
        part = block_list.shape[1]
        listed = jnp.pad(block_list.transpose(0, 2, 1), ((0, 1), (0, 0), (0, LANES - part)))
        tails = context_len.transpose(1, 0)[None] - (slots // micros - 1) * block_len
        listed = listed + jnp.pad(tails, ((micros, 0), (0, 1), (0, LANES - micros)))
        packed = pl.pallas_call(
            functools.partial(pack_kernel, part),
            out_shape=message,
            in_specs=[vmem] * 2,
            out_specs=vmem,
            scratch_shapes=[pltpu.VMEM(query.shape, F32)],
            compiler_params=params,
        )(query, listed)
        own = exchange(packed, "zy")
        sibling = lax.ppermute(own, "c", swap)
        rows = own[:, heads, 0]
        rows = exchange(
            jnp.broadcast_to(rows[None], (2 * tensor, planes, LANES)), ("c", "tp")
        )
    with jax.named_scope("block_attention"):
        me = (lax.axis_index("zy") * 2 + lax.axis_index("c")).astype(jnp.int32).reshape(1)
        mine, theirs = pl.pallas_call(
            functools.partial(holder_kernel, heads, scale, tensor, per),
            out_shape=(message, message),
            in_specs=[pl.BlockSpec(memory_space=pltpu.SMEM)] + [vmem] * 3 + [hbm] * 2,
            out_specs=(pl.BlockSpec(memory_space=pl.ANY),) * 2,
            scratch_shapes=[
                pltpu.VMEM(key_pool.shape, BF16),
                pltpu.VMEM(value_pool.shape, BF16),
                pltpu.VMEM((2 * planes, heads + 1, micros, LANES), BF16),
                pltpu.VMEM((2 * planes * 8, LANES), F32),
                pltpu.VMEM((2 * planes, 2, LANES), F32),
                pltpu.VMEM((8, LANES), jnp.int32),
                pltpu.SMEM((8, LANES), jnp.int32),
                pltpu.SemaphoreType.DMA((2,)),
                pltpu.SemaphoreType.DMA,
            ],
            compiler_params=large,
        )(me, own, sibling, rows, key_pool, value_pool)
    with jax.named_scope("parts_to_owners"):
        other = lax.ppermute(theirs, "c", swap)
        merged = pl.pallas_call(
            functools.partial(merge_kernel, heads),
            out_shape=message,
            in_specs=[vmem, vmem],
            out_specs=vmem,
            compiler_params=params,
        )(mine, other)
        arrived = exchange(merged, "zy")
    with jax.named_scope("owner_sum"):
        out = pl.pallas_call(
            functools.partial(owner_kernel, heads, scale),
            out_shape=jax.ShapeDtypeStruct(query.shape, BF16),
            in_specs=[vmem] * 4,
            out_specs=vmem,
            scratch_shapes=[
                pltpu.VMEM(query.shape, F32),
            ],
            compiler_params=params,
        )(arrived, query, new_token_keys.reshape(micros, dim), new_token_values.reshape(micros, dim))
        return out.transpose(1, 0, 2).reshape(micros, 1, width)


def solution(mesh):
    spread, tensor = mesh.devices.shape
    finer = Mesh(mesh.devices.reshape(spread // 2, 2, tensor), ("zy", "c", "tp"))
    dp = ("zy", "c")
    placed = (
        P(None, dp, "tp"),
        P(None, dp, "tp"),
        P(None, dp, "tp"),
        P(dp, None, "tp"),
        P(dp, None, "tp"),
        P(None, ("zy", "c", "tp"), None),
        P(None, dp),
    )
    return jax.shard_map(
        per_device, mesh=finer, in_specs=placed, out_specs=P(None, dp, "tp"), check_vma=False
    )
```

```python
import functools

import jax
import jax.numpy as jnp
from jax import lax
from jax.experimental import pallas as pl
from jax.experimental.pallas import tpu as pltpu
from jax.sharding import Mesh, PartitionSpec as P

LANES = 128
FIELD = 16
SPAN = 32
EMPTY = -1e30
PARTS = 3
F32, BF16 = jnp.float32, jnp.bfloat16


def lane_ids(shape):
    return lax.broadcasted_iota(jnp.int32, shape, len(shape) - 1)


def split3(x):
    high = x.astype(BF16).astype(F32)
    rest = x - high
    middle = rest.astype(BF16).astype(F32)
    return high, middle, rest - middle


def spread_levels(rows, groups):
    count = rows.shape[0] // 2
    line = lax.broadcasted_iota(jnp.int32, (8 * count, 2 * count), 0)
    source = lax.broadcasted_iota(jnp.int32, (8 * count, 2 * count), 1)
    pick = (source == (line // 8) * 2).astype(F32).astype(BF16)
    copies = jnp.dot(pick, rows, preferred_element_type=F32)
    sublane = lax.broadcasted_iota(jnp.int32, copies.shape, 0) % 8
    copies = jnp.where(lane_ids(copies.shape) // FIELD == sublane, copies, 0.0).astype(BF16)
    at = lax.broadcasted_iota(jnp.int32, (LANES, groups * LANES), 0) % FIELD // PARTS
    group = lane_ids((LANES, groups * LANES)) // LANES
    add = (at == group).astype(F32).astype(BF16)
    levels = jnp.dot(copies, add, preferred_element_type=F32)
    return [levels[:, g * LANES : (g + 1) * LANES] for g in range(groups)]


def pack_kernel(
    first_tail, query_hbm, list_hbm, length_hbm, out_ref, query_ref, list_ref, length_ref,
    wide, rows, sems,
):
    heads, micros, _ = query_ref.shape
    per = list_ref.shape[2]
    loads = [
        pltpu.make_async_copy(query_hbm, query_ref, sems.at[0]),
        pltpu.make_async_copy(list_hbm, list_ref, sems.at[1]),
        pltpu.make_async_copy(length_hbm, length_ref, sems.at[2]),
    ]
    for load in loads:
        load.start()
    rows[...] = jnp.zeros(rows.shape, F32)
    for load in loads:
        load.wait()
    wide[...] = query_ref[...].astype(F32)
    query = jnp.concatenate([wide[:, m, :] for m in range(micros)], axis=0).astype(BF16)
    for m in range(micros):
        rows[2 * m : 2 * m + 2, :per] = list_ref[m].astype(F32)
    rows[2 * micros : 2 * micros + 1, :micros] = (length_ref[...] - first_tail).astype(F32)
    row = pltpu.roll(rows[2 * micros : 2 * micros + 1, :], 2 * FIELD, 1)
    for m in range(micros):
        for field in range(2):
            at = 2 * m + field
            shift = field * FIELD + m * per
            entry = rows[at : at + 1, :]
            row = row + (pltpu.roll(entry, shift, 1) if shift else entry)
    listed = jnp.concatenate([row, jnp.zeros((1, LANES), F32)], axis=0).astype(BF16)
    message = jnp.concatenate([query.reshape(heads, micros, LANES), listed[None]], axis=0)
    out_ref[...] = jnp.broadcast_to(message[None], out_ref.shape)


def holder_kernel(
    heads, scale, tensor, per, me, own_ref, entry_ref, key_ref, value_ref, sib_key_ref,
    sib_value_ref, out_ref, keys, values, mixed, levels, pad, found, spots, sems, spot_sem,
):
    ranks = own_ref.shape[0]
    slots, block_len, _ = keys.shape
    entries = slots
    per_micro = entries // 2
    groups = 2 * heads // 8
    loads = [
        pltpu.make_async_copy(key_ref, keys, sems.at[0]),
        pltpu.make_async_copy(value_ref, values, sems.at[1]),
    ]
    for load in loads:
        load.start()
    pools = ((sib_key_ref, sib_value_ref), (keys, values))

    lane = lane_ids((ranks, LANES))
    listed = jnp.zeros((ranks, LANES), F32)
    for t in range(tensor):
        quarter = entry_ref[t].astype(F32)
        if t == 0:
            tails = quarter
        moved = pltpu.roll(quarter, t * SPAN, 1) if t else quarter
        listed = jnp.where(lane // SPAN == t, moved, listed)
    index = lane % FIELD
    order = (index // (per // 2)) * per_micro + (lane // SPAN) * (per // 2) + index % (per // 2)
    place = (lane % SPAN < per) & (lane < tensor * SPAN)
    slot = pltpu.roll(listed, LANES - FIELD, 1)
    code = slot * entries + order.astype(F32)
    firsts, lasts = [], []
    for holder in (me[0] + 1 - 2 * (me[0] % 2), me[0]):
        here = (listed == holder.astype(F32)) & place
        firsts.append(jnp.min(jnp.where(here, code, 1e6), axis=1, keepdims=True))
        lasts.append(jnp.max(jnp.where(here, code, -1.0), axis=1, keepdims=True))
    second = lane >= LANES // 2
    first = jnp.where(second, firsts[1], firsts[0])
    last = jnp.where(second, lasts[1], lasts[0])
    valid = last >= 0.0
    row = lax.broadcasted_iota(jnp.int32, (ranks, ranks), 0)
    ahead = lax.broadcasted_iota(jnp.int32, (ranks, ranks), 1)
    before = jnp.dot(
        (ahead < row).astype(F32).astype(BF16),
        valid.astype(F32).astype(BF16),
        preferred_element_type=F32,
    )
    chosen = valid & (before == (lane % (LANES // 2)).astype(F32))
    rank = lax.broadcasted_iota(jnp.int32, (ranks, LANES), 0).astype(F32)
    tail0 = jnp.sum(jnp.where(lane == 2 * FIELD, tails, 0.0), axis=1, keepdims=True)
    tail1 = jnp.sum(jnp.where(lane == 2 * FIELD + 1, tails, 0.0), axis=1, keepdims=True)

    def listing(x):
        return jnp.sum(jnp.where(chosen, x, 0.0), axis=0, keepdims=True)

    lines = [listing(x) for x in (rank, first, last, tail0, tail1)]
    lines[0] = jnp.where(listing(1.0) > 0.0, lines[0], float(ranks))
    lines.append(jnp.sum(valid.astype(F32), axis=0, keepdims=True))
    lines.append(jnp.zeros((8 - len(lines), LANES), F32))
    found[...] = jnp.concatenate(lines, axis=0).astype(jnp.int32)
    move = pltpu.make_async_copy(found, spots, spot_sem)
    move.start()
    mixed[...] = jnp.zeros(mixed.shape, F32)
    levels[...] = jnp.full(levels.shape, EMPTY, F32)
    pad[...] = jnp.zeros(pad.shape, F32)
    move.wait()

    together = min(4, slots // 2)
    token = lane_ids((heads, block_len))

    def step(pool, i, carry):
        work = []
        for k in range(together):
            n = pool * (LANES // 2) + i * together + k
            where = spots[0, n]
            for line in (1, 2):
                block = spots[line, n]
                at = block % entries
                micro = at // per_micro
                tail = jnp.where(micro == 0, spots[3, n], spots[4, n])
                live = jnp.where(at % per_micro == per_micro - 1, tail, block_len)
                work.append((where, block // entries, micro, live))
        olds = [(mixed[work[2 * k][0]], levels[work[2 * k][0]]) for k in range(together)]
        scores = []
        for where, block, micro, live in work:
            inner = pl.ds(micro * (heads // 2), heads // 2)
            query = own_ref[jnp.minimum(where, ranks - 1), inner].reshape(heads, LANES)
            score = lax.dot_general(
                query, pools[pool][0][block], (((1,), (1,)), ((), ())), preferred_element_type=F32
            )
            scores.append(jnp.where(token < live, score * scale, EMPTY))
        score = jnp.concatenate(scores, axis=0)
        peak = jnp.max(score, axis=1, keepdims=True)
        weight = jnp.exp(score - peak)
        total = jnp.sum(weight, axis=1, keepdims=True)
        weight = weight.astype(BF16)
        share = 1.0 / total
        level = peak + jnp.log(total)
        outs = []
        for k, (where, block, micro, live) in enumerate(work):
            part = jnp.dot(
                weight[k * heads : (k + 1) * heads],
                pools[pool][1][block],
                preferred_element_type=F32,
            )
            outs.append(part * share[k * heads : (k + 1) * heads])
        news = []
        for k in range(together):
            micro_a, micro_b = work[2 * k][2], work[2 * k + 1][2]
            level_a = level[2 * k * heads : (2 * k + 1) * heads]
            level_b = level[(2 * k + 1) * heads : (2 * k + 2) * heads]
            old_mixed, old_level = olds[k]
            for micro in range(2):
                rows = slice(micro * heads, (micro + 1) * heads)
                la = jnp.where(micro_a == micro, level_a, EMPTY)
                lb = jnp.where(micro_b == micro, level_b, EMPTY)
                top = jnp.maximum(old_level[rows], jnp.maximum(la, lb))
                wo = jnp.exp(old_level[rows] - top)
                wa = jnp.exp(la - top) * (micro_a == micro).astype(F32)
                wb = jnp.exp(lb - top) * (micro_b == micro).astype(F32)
                both = wo + wa + wb
                part = wo * old_mixed[rows] + wa * outs[2 * k] + wb * outs[2 * k + 1]
                news.append((work[2 * k][0], rows, part / both, top + jnp.log(both)))
        for where, rows, part, depth in news:
            mixed[where, rows] = part
            levels[where, rows] = depth
        return carry

    for pool in range(2):
        if pool == 1:
            for load in loads:
                load.wait()
        count = spots[5, pool * (LANES // 2)]
        steps = (count + together - 1) // together
        lax.fori_loop(0, steps, functools.partial(step, pool), 0)

    sublane = lax.broadcasted_iota(jnp.int32, (1, 8, LANES), 1)
    lane8 = lane_ids((1, 8, LANES))
    field = jnp.where(lane8 // FIELD == sublane, lane8 % FIELD, FIELD)
    tile = jnp.zeros((ranks, 8, LANES), F32)
    for g in range(groups):
        for j, term in enumerate(split3(levels[:ranks, 8 * g : 8 * (g + 1)])):
            tile = jnp.where(field == PARTS * g + j, term, tile)
    pad[:, 0, :] = jnp.sum(tile, axis=1)
    out_ref[:, heads] = pad[...].astype(BF16)
    out_ref[:, :heads] = mixed[:ranks].astype(BF16).reshape(ranks, heads, 2, LANES)


def owner_kernel(heads, scale, part_ref, query_ref, key_ref, value_ref, out_ref, wide):
    count = part_ref.shape[0]
    pieces = heads // 8
    groups = 2 * pieces
    wide[...] = query_ref[...].astype(F32)
    levels = spread_levels(part_ref[:, heads].reshape(2 * count, LANES), groups)
    for g in range(groups):
        micro, piece = g // pieces, g % pieces
        rows = slice(piece * 8, (piece + 1) * 8)
        key = key_ref[micro : micro + 1, :].astype(F32)
        own = jnp.sum(wide[rows, micro, :] * key, axis=1, keepdims=True) * scale
        level = levels[g].reshape(count, 8, LANES)
        top = jnp.maximum(jnp.max(level, axis=0), own)
        weight = jnp.exp(level - top[None])
        self_weight = jnp.exp(own - top)
        part = part_ref[:, 4 * g : 4 * (g + 1)].reshape(8 * count, LANES).astype(F32)
        mixed = jnp.sum(weight * part.reshape(count, 8, LANES), axis=0)
        mixed = mixed + self_weight * value_ref[micro : micro + 1, :].astype(F32)
        wide[rows, micro, :] = mixed / (jnp.sum(weight, axis=0) + self_weight)
    out_ref[...] = wide[...].astype(BF16)


def in_hbm(x):
    return pltpu.with_memory_space_constraint(x, pltpu.HBM)


def in_vmem(x):
    return pltpu.with_memory_space_constraint(x, pltpu.VMEM)


def exchange(x, axis):
    return lax.all_to_all(x, axis, 0, 0)


def per_device(
    queries, new_token_keys, new_token_values, key_pool, value_pool, block_list, context_len
):
    planes, tensor = lax.axis_size("zy"), lax.axis_size("tp")
    micros, _, width = queries.shape
    slots, block_len, dim = key_pool.shape
    heads = width // dim
    scale = dim ** (-0.5)
    per = slots // tensor
    swap = [(0, 1), (1, 0)]
    hbm = pl.BlockSpec(memory_space=pltpu.HBM)
    vmem = pl.BlockSpec(memory_space=pltpu.VMEM)
    params = pltpu.CompilerParams(vmem_limit_bytes=32 * 1024 * 1024)
    message = jax.ShapeDtypeStruct((planes, heads + 1, micros, LANES), BF16)
    query = queries.reshape(micros, heads, dim).transpose(1, 0, 2)

    with jax.named_scope("queries_to_holders"):
        listed, lengths = block_list.transpose(0, 2, 1), context_len.transpose(1, 0)
        packed = pl.pallas_call(
            functools.partial(pack_kernel, (slots // micros - 1) * block_len),
            out_shape=message,
            in_specs=[hbm] * 3,
            out_specs=vmem,
            scratch_shapes=[
                pltpu.VMEM(query.shape, BF16),
                pltpu.VMEM(listed.shape, jnp.int32),
                pltpu.VMEM(lengths.shape, jnp.int32),
                pltpu.VMEM(query.shape, F32),
                pltpu.VMEM((8, LANES), F32),
                pltpu.SemaphoreType.DMA((3,)),
            ],
            compiler_params=params,
        )(*(in_hbm(x) for x in (query, listed, lengths)))
        packed, key_pool, value_pool = lax.optimization_barrier((packed, key_pool, value_pool))
        own = exchange(packed, "zy")
        rows = own[:, heads, 0]
        rows = exchange(jnp.broadcast_to(rows[None], (tensor, planes, LANES)), "tp")
    with jax.named_scope("pools_of_both_cores"):
        sib_key = lax.ppermute(key_pool, "c", swap)
        sib_value = lax.ppermute(value_pool, "c", swap)
    with jax.named_scope("block_attention"):
        me = (lax.axis_index("zy") * 2 + lax.axis_index("c")).astype(jnp.int32).reshape(1)
        parts = pl.pallas_call(
            functools.partial(holder_kernel, heads, scale, tensor, per),
            out_shape=message,
            in_specs=[pl.BlockSpec(memory_space=pltpu.SMEM)] + [vmem] * 2 + [hbm] * 2 + [vmem] * 2,
            out_specs=vmem,
            scratch_shapes=[
                pltpu.VMEM(key_pool.shape, BF16),
                pltpu.VMEM(value_pool.shape, BF16),
                pltpu.VMEM((planes + 1, micros * heads, LANES), F32),
                pltpu.VMEM((planes + 1, micros * heads, LANES), F32),
                pltpu.VMEM((planes, 2, LANES), F32),
                pltpu.VMEM((8, LANES), jnp.int32),
                pltpu.SMEM((8, LANES), jnp.int32),
                pltpu.SemaphoreType.DMA((2,)),
                pltpu.SemaphoreType.DMA,
            ],
            compiler_params=params,
        )(me, own, rows, in_hbm(key_pool), in_hbm(value_pool), in_vmem(sib_key), in_vmem(sib_value))
    with jax.named_scope("parts_to_owners"):
        arrived = exchange(parts, "zy")
    with jax.named_scope("owner_sum"):
        out = pl.pallas_call(
            functools.partial(owner_kernel, heads, scale),
            out_shape=jax.ShapeDtypeStruct(query.shape, BF16),
            in_specs=[vmem] * 4,
            out_specs=vmem,
            scratch_shapes=[
                pltpu.VMEM(query.shape, F32),
            ],
            compiler_params=params,
        )(arrived, query, new_token_keys.reshape(micros, dim), new_token_values.reshape(micros, dim))
        return out.transpose(1, 0, 2).reshape(micros, 1, width)


def solution(mesh):
    spread, tensor = mesh.devices.shape
    finer = Mesh(mesh.devices.reshape(spread // 2, 2, tensor), ("zy", "c", "tp"))
    dp = ("zy", "c")
    placed = (
        P(None, dp, "tp"),
        P(None, dp, "tp"),
        P(None, dp, "tp"),
        P(dp, None, "tp"),
        P(dp, None, "tp"),
        P(None, ("zy", "c", "tp"), None),
        P(None, dp),
    )
    return jax.shard_map(
        per_device, mesh=finer, in_specs=placed, out_specs=P(None, dp, "tp"), check_vma=False
    )
```

```python
import functools

import jax
import jax.numpy as jnp
from jax import lax
from jax.experimental import pallas as pl
from jax.experimental.pallas import tpu as pltpu
from jax.sharding import Mesh, PartitionSpec as P

LANES = 128
COST = 10**11
FIELD = 16
SPAN = 32
EMPTY = -1e30
PARTS = 3
F32, BF16 = jnp.float32, jnp.bfloat16


def lane_ids(shape):
    return lax.broadcasted_iota(jnp.int32, shape, len(shape) - 1)


def split3(x):
    high = x.astype(BF16).astype(F32)
    rest = x - high
    middle = rest.astype(BF16).astype(F32)
    return high, middle, rest - middle


def spread_levels(rows, groups):
    count = rows.shape[0] // 2
    line = lax.broadcasted_iota(jnp.int32, (8 * count, 2 * count), 0)
    source = lax.broadcasted_iota(jnp.int32, (8 * count, 2 * count), 1)
    pick = (source == (line // 8) * 2).astype(F32).astype(BF16)
    copies = jnp.dot(pick, rows, preferred_element_type=F32)
    sublane = lax.broadcasted_iota(jnp.int32, copies.shape, 0) % 8
    copies = jnp.where(lane_ids(copies.shape) // FIELD == sublane, copies, 0.0).astype(BF16)
    at = lax.broadcasted_iota(jnp.int32, (LANES, groups * LANES), 0) % FIELD // PARTS
    group = lane_ids((LANES, groups * LANES)) // LANES
    add = (at == group).astype(F32).astype(BF16)
    levels = jnp.dot(copies, add, preferred_element_type=F32)
    return [levels[:, g * LANES : (g + 1) * LANES] for g in range(groups)]


def first_kernel(
    first_tail, query_hbm, list_hbm, length_hbm, copies_ref, query_ref, tail_ref,
    narrow, entries, lengths, wide, rows, sems,
):
    heads, micros, _ = narrow.shape
    loads = [
        pltpu.make_async_copy(list_hbm, entries, sems.at[0]),
        pltpu.make_async_copy(query_hbm, narrow, sems.at[1]),
        pltpu.make_async_copy(length_hbm, lengths, sems.at[2]),
    ]
    for load in loads:
        load.start()
    rows[...] = jnp.zeros(rows.shape, F32)
    loads[0].wait()
    copies_ref[...] = jnp.broadcast_to(entries[...][None], copies_ref.shape)
    loads[1].wait()
    wide[...] = narrow[...].astype(F32)
    query = jnp.concatenate([wide[:, m, :] for m in range(micros)], axis=0).astype(BF16)
    query_ref[...] = query.reshape(heads, micros, LANES)
    loads[2].wait()
    rows[0:1, :micros] = (lengths[...] - first_tail).astype(F32)
    tail_ref[...] = rows[...]


def pack_kernel(query_ref, list_ref, tail_ref, out_ref, rows):
    tensor, micros, _, part = list_ref.shape
    rows[...] = jnp.zeros(rows.shape, F32)
    fields = []
    for t in range(tensor):
        for m in range(micros):
            at = 2 * (t * micros + m)
            rows[at : at + 2, :part] = list_ref[t, m].astype(F32)
            fields.extend((at + field, t * SPAN + field * FIELD + m * part) for field in range(2))
    entries = rows[0:1, :]
    for line, shift in fields[1:]:
        entries = entries + pltpu.roll(rows[line : line + 1, :], shift, 1)
    listed = jnp.concatenate([entries, tail_ref[0:1, :]], axis=0).astype(BF16)
    message = jnp.concatenate([query_ref[...], listed[None]], axis=0)
    out_ref[...] = jnp.broadcast_to(message[None], out_ref.shape)


def find_kernel(tensor, per, me, own_ref, found_ref, pad):
    ranks, heads = own_ref.shape[0], own_ref.shape[1] - 1
    entries = tensor * per
    per_micro = entries // 2
    lane = lane_ids((ranks, LANES))
    pad[...] = own_ref[:, heads].astype(F32)
    listed = pad[:, 0, :]
    tails = pad[:, 1, :]
    index = lane % FIELD
    order = (index // (per // 2)) * per_micro + (lane // SPAN) * (per // 2) + index % (per // 2)
    place = (lane % SPAN < per) & (lane < tensor * SPAN)
    slot = pltpu.roll(listed, LANES - FIELD, 1)
    code = slot * entries + order.astype(F32)
    firsts, lasts = [], []
    for holder in (me[0] + 1 - 2 * (me[0] % 2), me[0]):
        here = (listed == holder.astype(F32)) & place
        firsts.append(jnp.min(jnp.where(here, code, 1e6), axis=1, keepdims=True))
        lasts.append(jnp.max(jnp.where(here, code, -1.0), axis=1, keepdims=True))
    second = lane >= LANES // 2
    first = jnp.where(second, firsts[1], firsts[0])
    last = jnp.where(second, lasts[1], lasts[0])
    valid = last >= 0.0
    row = lax.broadcasted_iota(jnp.int32, (ranks, ranks), 0)
    ahead = lax.broadcasted_iota(jnp.int32, (ranks, ranks), 1)
    before = jnp.dot(
        (ahead < row).astype(F32).astype(BF16),
        valid.astype(F32).astype(BF16),
        preferred_element_type=F32,
    )
    chosen = valid & (before == (lane % (LANES // 2)).astype(F32))
    rank = lax.broadcasted_iota(jnp.int32, (ranks, LANES), 0).astype(F32)
    tail0 = jnp.sum(jnp.where(lane == 0, tails, 0.0), axis=1, keepdims=True)
    tail1 = jnp.sum(jnp.where(lane == 1, tails, 0.0), axis=1, keepdims=True)

    def listing(x):
        return jnp.sum(jnp.where(chosen, x, 0.0), axis=0, keepdims=True)

    lines = [listing(x) for x in (rank, first, last, tail0, tail1)]
    lines[0] = jnp.where(listing(1.0) > 0.0, lines[0], float(ranks))
    lines.append(jnp.sum(valid.astype(F32), axis=0, keepdims=True))
    lines.append(jnp.zeros((8 - len(lines), LANES), F32))
    found_ref[...] = jnp.concatenate(lines, axis=0).astype(jnp.int32)


def holder_kernel(
    heads, scale, own_ref, found_ref, key_ref, value_ref, sib_key_ref, sib_value_ref,
    out_ref, keys, values, mixed, levels, tiles, pad, spots, sems, spot_sem,
):
    ranks = own_ref.shape[0]
    slots, block_len, _ = keys.shape
    entries = slots
    per_micro = entries // 2
    groups = 2 * heads // 8
    move = pltpu.make_async_copy(found_ref, spots, spot_sem)
    move.start()
    loads = [
        pltpu.make_async_copy(key_ref, keys, sems.at[0]),
        pltpu.make_async_copy(value_ref, values, sems.at[1]),
    ]
    for load in loads:
        load.start()
    pools = ((sib_key_ref, sib_value_ref), (keys, values))
    mixed[...] = jnp.zeros(mixed.shape, F32)
    levels[...] = jnp.full(levels.shape, EMPTY, F32)
    pad[...] = jnp.zeros(pad.shape, F32)
    lane8 = lane_ids((8, LANES))
    sublane = lax.broadcasted_iota(jnp.int32, (8, LANES), 0)
    field = jnp.where(lane8 // FIELD == sublane, lane8 % FIELD, FIELD)
    blank = jnp.where(field < PARTS * groups, EMPTY, 0.0)
    tiles[...] = jnp.broadcast_to(blank[None], tiles.shape)
    move.wait()

    together = min(8, slots // 2)
    token = lane_ids((heads, block_len))

    def step(pool, i, carry):
        work = []
        for k in range(together):
            n = pool * (LANES // 2) + i * together + k
            where = spots[0, n]
            for line in (1, 2):
                block = spots[line, n]
                at = block % entries
                micro = at // per_micro
                tail = jnp.where(micro == 0, spots[3, n], spots[4, n])
                live = jnp.where(at % per_micro == per_micro - 1, tail, block_len)
                work.append((where, block // entries, micro, live))
        olds = [(mixed[work[2 * k][0]], levels[work[2 * k][0]]) for k in range(together)]
        scores = []
        for where, block, micro, live in work:
            inner = pl.ds(micro * (heads // 2), heads // 2)
            query = own_ref[jnp.minimum(where, ranks - 1), inner].reshape(heads, LANES)
            score = lax.dot_general(
                query, pools[pool][0][block], (((1,), (1,)), ((), ())), preferred_element_type=F32
            )
            scores.append(jnp.where(token < live, score * scale, EMPTY))
        score = jnp.concatenate(scores, axis=0)
        peak = jnp.max(score, axis=1, keepdims=True)
        weight = jnp.exp(score - peak)
        total = jnp.sum(weight, axis=1, keepdims=True)
        weight = weight.astype(BF16)
        share = 1.0 / total
        level = peak + jnp.log(total)
        outs = []
        for k, (where, block, micro, live) in enumerate(work):
            part = jnp.dot(
                weight[k * heads : (k + 1) * heads],
                pools[pool][1][block],
                preferred_element_type=F32,
            )
            outs.append(part * share[k * heads : (k + 1) * heads])
        news, made = [], []
        for k in range(together):
            micro_a, micro_b = work[2 * k][2], work[2 * k + 1][2]
            level_a = level[2 * k * heads : (2 * k + 1) * heads]
            level_b = level[(2 * k + 1) * heads : (2 * k + 2) * heads]
            old_mixed, old_level = olds[k]
            tile = jnp.zeros((8, LANES), F32)
            for micro in range(2):
                rows = slice(micro * heads, (micro + 1) * heads)
                la = jnp.where(micro_a == micro, level_a, EMPTY)
                lb = jnp.where(micro_b == micro, level_b, EMPTY)
                top = jnp.maximum(old_level[rows], jnp.maximum(la, lb))
                wo = jnp.exp(old_level[rows] - top)
                wa = jnp.exp(la - top) * (micro_a == micro).astype(F32)
                wb = jnp.exp(lb - top) * (micro_b == micro).astype(F32)
                both = wo + wa + wb
                part = wo * old_mixed[rows] + wa * outs[2 * k] + wb * outs[2 * k + 1]
                depth = top + jnp.log(both)
                news.append((work[2 * k][0], rows, part / both, depth))
                for piece in range(heads // 8):
                    group = micro * (heads // 8) + piece
                    for j, term in enumerate(split3(depth[piece * 8 : (piece + 1) * 8])):
                        tile = jnp.where(field == PARTS * group + j, term, tile)
            made.append((work[2 * k][0], tile))
        for where, rows, part, depth in news:
            mixed[where, rows] = part
            levels[where, rows] = depth
        for where, tile in made:
            tiles[where] = tile
        return carry

    for pool in range(2):
        if pool == 1:
            for load in loads:
                load.wait()
        count = spots[5, pool * (LANES // 2)]
        steps = (count + together - 1) // together
        lax.fori_loop(0, steps, functools.partial(step, pool), 0)

    pad[:, 0, :] = jnp.sum(tiles[:ranks], axis=1)
    out_ref[:, heads] = pad[...].astype(BF16)
    out_ref[:, :heads] = mixed[:ranks].astype(BF16).reshape(ranks, heads, 2, LANES)


def owner_kernel(heads, scale, part_ref, query_ref, key_ref, value_ref, out_ref, wide):
    count = part_ref.shape[0]
    pieces = heads // 8
    groups = 2 * pieces
    wide[...] = query_ref[...].astype(F32)
    levels = spread_levels(part_ref[:, heads].reshape(2 * count, LANES), groups)
    for g in range(groups):
        micro, piece = g // pieces, g % pieces
        rows = slice(piece * 8, (piece + 1) * 8)
        key = key_ref[micro : micro + 1, :].astype(F32)
        own = jnp.sum(wide[rows, micro, :] * key, axis=1, keepdims=True) * scale
        level = levels[g].reshape(count, 8, LANES)
        top = jnp.maximum(jnp.max(level, axis=0), own)
        weight = jnp.exp(level - top[None])
        self_weight = jnp.exp(own - top)
        part = part_ref[:, 4 * g : 4 * (g + 1)].reshape(8 * count, LANES).astype(F32)
        mixed = jnp.sum(weight * part.reshape(count, 8, LANES), axis=0)
        mixed = mixed + self_weight * value_ref[micro : micro + 1, :].astype(F32)
        wide[rows, micro, :] = mixed / (jnp.sum(weight, axis=0) + self_weight)
    out_ref[...] = wide[...].astype(BF16)


def in_hbm(x):
    return pltpu.with_memory_space_constraint(x, pltpu.HBM)


def in_vmem(x):
    return pltpu.with_memory_space_constraint(x, pltpu.VMEM)


def exchange(x, axis):
    return lax.all_to_all(x, axis, 0, 0)


def per_device(
    queries, new_token_keys, new_token_values, key_pool, value_pool, block_list, context_len
):
    planes, tensor = lax.axis_size("zy"), lax.axis_size("tp")
    micros, _, width = queries.shape
    slots, block_len, dim = key_pool.shape
    heads = width // dim
    scale = dim ** (-0.5)
    per = slots // tensor
    swap = [(0, 1), (1, 0)]
    hbm = pl.BlockSpec(memory_space=pltpu.HBM)
    vmem = pl.BlockSpec(memory_space=pltpu.VMEM)
    params = pltpu.CompilerParams(vmem_limit_bytes=32 * 1024 * 1024)
    message = jax.ShapeDtypeStruct((planes, heads + 1, micros, LANES), BF16)
    query = queries.reshape(micros, heads, dim).transpose(1, 0, 2)

    with jax.named_scope("queries_to_holders"):
        listed, lengths = block_list.transpose(0, 2, 1), context_len.transpose(1, 0)
        copies, ordered, tails = pl.pallas_call(
            functools.partial(first_kernel, (slots // micros - 1) * block_len),
            out_shape=(
                jax.ShapeDtypeStruct((tensor, *listed.shape), jnp.int32),
                jax.ShapeDtypeStruct(query.shape, BF16),
                jax.ShapeDtypeStruct((8, LANES), F32),
            ),
            in_specs=[hbm] * 3,
            out_specs=(vmem,) * 3,
            scratch_shapes=[
                pltpu.VMEM(query.shape, BF16),
                pltpu.VMEM(listed.shape, jnp.int32),
                pltpu.VMEM(lengths.shape, jnp.int32),
                pltpu.VMEM(query.shape, F32),
                pltpu.VMEM((8, LANES), F32),
                pltpu.SemaphoreType.DMA((3,)),
            ],
            compiler_params=params,
        )(in_hbm(query), in_hbm(listed), in_hbm(lengths))
        packed = pl.pallas_call(
            pack_kernel,
            out_shape=message,
            in_specs=[vmem] * 3,
            out_specs=vmem,
            scratch_shapes=[pltpu.VMEM((2 * tensor * micros, LANES), F32)],
            compiler_params=params,
        )(ordered, exchange(copies, "tp"), tails)
        own = exchange(packed, "zy")
    with jax.named_scope("pools_of_both_cores"):
        sib_key = lax.ppermute(key_pool, "c", swap)
        sib_value = lax.ppermute(value_pool, "c", swap)
    with jax.named_scope("block_attention"):
        me = (lax.axis_index("zy") * 2 + lax.axis_index("c")).astype(jnp.int32).reshape(1)
        found = pl.pallas_call(
            functools.partial(find_kernel, tensor, per),
            out_shape=jax.ShapeDtypeStruct((8, LANES), jnp.int32),
            in_specs=[pl.BlockSpec(memory_space=pltpu.SMEM), vmem],
            out_specs=vmem,
            scratch_shapes=[pltpu.VMEM((planes, 2, LANES), F32)],
            compiler_params=params,
            cost_estimate=pl.CostEstimate(
                flops=COST, bytes_accessed=2 * own.size, transcendentals=0
            ),
        )(me, own)
        parts = pl.pallas_call(
            functools.partial(holder_kernel, heads, scale),
            out_shape=message,
            in_specs=[vmem] * 2 + [hbm] * 2 + [vmem] * 2,
            out_specs=vmem,
            scratch_shapes=[
                pltpu.VMEM(key_pool.shape, BF16),
                pltpu.VMEM(value_pool.shape, BF16),
                pltpu.VMEM((planes + 1, micros * heads, LANES), F32),
                pltpu.VMEM((planes + 1, micros * heads, LANES), F32),
                pltpu.VMEM((planes + 1, 8, LANES), F32),
                pltpu.VMEM((planes, 2, LANES), F32),
                pltpu.SMEM((8, LANES), jnp.int32),
                pltpu.SemaphoreType.DMA((2,)),
                pltpu.SemaphoreType.DMA,
            ],
            compiler_params=params,
        )(own, found, in_hbm(key_pool), in_hbm(value_pool), in_vmem(sib_key), in_vmem(sib_value))
    with jax.named_scope("parts_to_owners"):
        arrived = exchange(parts, "zy")
    with jax.named_scope("owner_sum"):
        out = pl.pallas_call(
            functools.partial(owner_kernel, heads, scale),
            out_shape=jax.ShapeDtypeStruct(query.shape, BF16),
            in_specs=[vmem] * 4,
            out_specs=vmem,
            scratch_shapes=[
                pltpu.VMEM(query.shape, F32),
            ],
            compiler_params=params,
        )(arrived, query, new_token_keys.reshape(micros, dim), new_token_values.reshape(micros, dim))
        return out.transpose(1, 0, 2).reshape(micros, 1, width)


def solution(mesh):
    spread, tensor = mesh.devices.shape
    finer = Mesh(mesh.devices.reshape(spread // 2, 2, tensor), ("zy", "c", "tp"))
    dp = ("zy", "c")
    placed = (
        P(None, dp, "tp"),
        P(None, dp, "tp"),
        P(None, dp, "tp"),
        P(dp, None, "tp"),
        P(dp, None, "tp"),
        P(None, ("zy", "c", "tp"), None),
        P(None, dp),
    )
    return jax.shard_map(
        per_device, mesh=finer, in_specs=placed, out_specs=P(None, dp, "tp"), check_vma=False
    )
```

```python
import functools

import jax
import jax.numpy as jnp
from jax import lax
from jax.experimental import pallas as pl
from jax.experimental.pallas import tpu as pltpu
from jax.sharding import Mesh, PartitionSpec as P

LANES = 128
COST = 10**11
FIELD = 16
SPAN = 32
EMPTY = -1e30
PARTS = 3
F32, BF16 = jnp.float32, jnp.bfloat16


def lane_ids(shape):
    return lax.broadcasted_iota(jnp.int32, shape, len(shape) - 1)


def split3(x):
    high = x.astype(BF16).astype(F32)
    rest = x - high
    middle = rest.astype(BF16).astype(F32)
    return high, middle, rest - middle


def spread_levels(rows, groups):
    count = rows.shape[0] // 2
    line = lax.broadcasted_iota(jnp.int32, (8 * count, 2 * count), 0)
    source = lax.broadcasted_iota(jnp.int32, (8 * count, 2 * count), 1)
    pick = (source == (line // 8) * 2).astype(F32).astype(BF16)
    copies = jnp.dot(pick, rows, preferred_element_type=F32)
    sublane = lax.broadcasted_iota(jnp.int32, copies.shape, 0) % 8
    copies = jnp.where(lane_ids(copies.shape) // FIELD == sublane, copies, 0.0).astype(BF16)
    at = lax.broadcasted_iota(jnp.int32, (LANES, groups * LANES), 0) % FIELD // PARTS
    group = lane_ids((LANES, groups * LANES)) // LANES
    add = (at == group).astype(F32).astype(BF16)
    levels = jnp.dot(copies, add, preferred_element_type=F32)
    return [levels[:, g * LANES : (g + 1) * LANES] for g in range(groups)]


def first_kernel(
    first_tail, query_hbm, list_hbm, length_hbm, copies_ref, query_ref, tail_ref,
    narrow, entries, lengths, wide, rows, sems,
):
    heads, micros, _ = narrow.shape
    loads = [
        pltpu.make_async_copy(list_hbm, entries, sems.at[0]),
        pltpu.make_async_copy(query_hbm, narrow, sems.at[1]),
        pltpu.make_async_copy(length_hbm, lengths, sems.at[2]),
    ]
    for load in loads:
        load.start()
    rows[...] = jnp.zeros(rows.shape, F32)
    loads[0].wait()
    copies_ref[...] = jnp.broadcast_to(entries[...][None], copies_ref.shape)
    loads[1].wait()
    wide[...] = narrow[...].astype(F32)
    query = jnp.concatenate([wide[:, m, :] for m in range(micros)], axis=0).astype(BF16)
    query_ref[...] = query.reshape(heads, micros, LANES)
    loads[2].wait()
    rows[0:1, :micros] = (lengths[...] - first_tail).astype(F32)
    tail_ref[...] = rows[...]


def pack_kernel(query_ref, list_ref, tail_ref, out_ref, rows):
    tensor, micros, _, part = list_ref.shape
    rows[...] = jnp.zeros(rows.shape, F32)
    fields = []
    for t in range(tensor):
        for m in range(micros):
            at = 2 * (t * micros + m)
            rows[at : at + 2, :part] = list_ref[t, m].astype(F32)
            fields.extend((at + field, t * SPAN + field * FIELD + m * part) for field in range(2))
    entries = rows[0:1, :]
    for line, shift in fields[1:]:
        entries = entries + pltpu.roll(rows[line : line + 1, :], shift, 1)
    listed = jnp.concatenate([entries, tail_ref[0:1, :]], axis=0).astype(BF16)
    message = jnp.concatenate([query_ref[...], listed[None]], axis=0)
    out_ref[...] = jnp.broadcast_to(message[None], out_ref.shape)


def find_kernel(tensor, per, block_len, me, own_ref, found_ref, pad):
    ranks, heads = own_ref.shape[0], own_ref.shape[1] - 1
    entries = tensor * per
    per_micro = entries // 2
    lane = lane_ids((ranks, LANES))
    pad[...] = own_ref[:, heads].astype(F32)
    listed = pad[:, 0, :]
    tails = pad[:, 1, :]
    index = lane % FIELD
    order = (index // (per // 2)) * per_micro + (lane // SPAN) * (per // 2) + index % (per // 2)
    place = (lane % SPAN < per) & (lane < tensor * SPAN)
    slot = pltpu.roll(listed, LANES - FIELD, 1)
    code = slot * entries + order.astype(F32)
    firsts, lasts = [], []
    for holder in (me[0] + 1 - 2 * (me[0] % 2), me[0]):
        here = (listed == holder.astype(F32)) & place
        firsts.append(jnp.min(jnp.where(here, code, 1e6), axis=1, keepdims=True))
        lasts.append(jnp.max(jnp.where(here, code, -1.0), axis=1, keepdims=True))
    second = lane >= LANES // 2
    first = jnp.where(second, firsts[1], firsts[0])
    last = jnp.where(second, lasts[1], lasts[0])
    valid = last >= 0.0
    row = lax.broadcasted_iota(jnp.int32, (ranks, ranks), 0)
    ahead = lax.broadcasted_iota(jnp.int32, (ranks, ranks), 1)
    before = jnp.dot(
        (ahead < row).astype(F32).astype(BF16),
        valid.astype(F32).astype(BF16),
        preferred_element_type=F32,
    )
    chosen = valid & (before == (lane % (LANES // 2)).astype(F32))
    rank = lax.broadcasted_iota(jnp.int32, (ranks, LANES), 0).astype(F32)
    tail0 = jnp.sum(jnp.where(lane == 0, tails, 0.0), axis=1, keepdims=True)
    tail1 = jnp.sum(jnp.where(lane == 1, tails, 0.0), axis=1, keepdims=True)

    def listing(x):
        return jnp.sum(jnp.where(chosen, x, 0.0), axis=0, keepdims=True)

    lines = [listing(x) for x in (rank, first, last, tail0, tail1)]
    lines[0] = jnp.where(listing(1.0) > 0.0, lines[0], float(ranks))
    lines.append(jnp.sum(valid.astype(F32), axis=0, keepdims=True))
    ranked, code_a, code_b, left0, left1, count = (x.astype(jnp.int32) for x in lines)
    places, micros, lives = [], [], []
    for code in (code_a, code_b):
        at = code % entries
        micro = at // per_micro
        left = jnp.where(micro == 0, left0, left1)
        places.append(code // entries)
        micros.append(micro)
        lives.append(jnp.where(at % per_micro == per_micro - 1, left, block_len))
    found_ref[...] = jnp.concatenate([ranked, *places, *micros, *lives, count], axis=0)


def holder_kernel(
    heads, scale, own_ref, found_ref, key_ref, value_ref, sib_key_ref, sib_value_ref,
    out_ref, keys, values, tops, sums, mixed, parts, tiles, pad, spots, sems, spot_sem,
):
    ranks = own_ref.shape[0]
    slots, block_len, _ = keys.shape
    groups = 2 * heads // 8
    move = pltpu.make_async_copy(found_ref, spots, spot_sem)
    move.start()
    loads = [
        pltpu.make_async_copy(key_ref, keys, sems.at[0]),
        pltpu.make_async_copy(value_ref, values, sems.at[1]),
    ]
    for load in loads:
        load.start()
    pools = ((sib_key_ref, sib_value_ref), (keys, values))
    tops[...] = jnp.full(tops.shape, EMPTY, F32)
    sums[...] = jnp.zeros(sums.shape, F32)
    mixed[...] = jnp.zeros(mixed.shape, F32)
    parts[...] = jnp.zeros(parts.shape, F32)
    pad[...] = jnp.zeros(pad.shape, F32)
    lane8 = lane_ids((8, LANES))
    sublane = lax.broadcasted_iota(jnp.int32, (8, LANES), 0)
    field = jnp.where(lane8 // FIELD == sublane, lane8 % FIELD, FIELD)
    half = PARTS * groups // 2
    for micro in range(2):
        blank = jnp.where((field >= micro * half) & (field < (micro + 1) * half), EMPTY, 0.0)
        tiles[:, micro] = jnp.broadcast_to(blank[None], (ranks + 1, 8, LANES))
    move.wait()

    together = min(10, slots // 2)
    token = lane_ids((heads, block_len))

    def step(pool, i, carry):
        work = []
        for k in range(together):
            n = pool * (LANES // 2) + i * together + k
            where = spots[0, n]
            for line in range(2):
                work.append((where, spots[1 + line, n], spots[3 + line, n], spots[5 + line, n]))
        scores = []
        for k in range(together):
            pair = work[2 * k : 2 * k + 2]
            queries = []
            for where, block, micro, live in pair:
                inner = pl.ds(micro * (heads // 2), heads // 2)
                query = own_ref[jnp.minimum(where, ranks - 1), inner].reshape(heads, LANES)
                queries.append(query)
            both = lax.dot_general(
                jnp.concatenate(queries, axis=0),
                jnp.concatenate([pools[pool][0][block] for _, block, _, _ in pair], axis=0),
                (((1,), (1,)), ((), ())),
                preferred_element_type=F32,
            )
            for line, (where, block, micro, live) in enumerate(pair):
                score = both[line * heads : (line + 1) * heads, line * block_len : (line + 1) * block_len]
                scores.append(jnp.where(token < live, score * scale, EMPTY))
        score = jnp.concatenate(scores, axis=0)
        peak = jnp.max(score, axis=1, keepdims=True)
        weight = jnp.exp(score - peak)
        total = jnp.sum(weight, axis=1, keepdims=True)
        weight = weight.astype(BF16)
        nothing = jnp.zeros((heads, block_len), BF16)
        mixes = []
        for k in range(together):
            wa = weight[2 * k * heads : (2 * k + 1) * heads]
            wb = weight[(2 * k + 1) * heads : (2 * k + 2) * heads]
            spread = jnp.concatenate(
                [
                    jnp.concatenate([wa, nothing], axis=1),
                    jnp.concatenate([nothing, wb], axis=1),
                ],
                axis=0,
            )
            pair = jnp.concatenate(
                [pools[pool][1][work[2 * k][1]], pools[pool][1][work[2 * k + 1][1]]], axis=0
            )
            mixes.append(jnp.dot(spread, pair, preferred_element_type=F32))
        for line in range(2):
            olds = []
            for where, block, micro, live in work[line::2]:
                olds.append((tops[where, micro], sums[where, micro], mixed[where, micro]))
            news = []
            for k, (where, block, micro, live) in enumerate(work[line::2]):
                rows = slice((2 * k + line) * heads, (2 * k + line + 1) * heads)
                part = mixes[k][line * heads : (line + 1) * heads]
                old_top, old_sum, old_mixed = olds[k]
                top = jnp.maximum(old_top, peak[rows])
                old_scale, scale_here = jnp.exp(old_top - top), jnp.exp(peak[rows] - top)
                new_sum = old_scale * old_sum + scale_here * total[rows]
                new_mixed = old_scale * old_mixed + scale_here * part
                depth = top + jnp.log(new_sum)
                tile = jnp.zeros((8, LANES), F32)
                for piece in range(heads // 8):
                    for j, term in enumerate(split3(depth[piece * 8 : (piece + 1) * 8])):
                        tile = jnp.where(field == PARTS * piece + j + micro * half, term, tile)
                news.append((where, micro, top, new_sum, new_mixed, new_mixed / new_sum, tile))
            for where, micro, top, new_sum, new_mixed, part, tile in news:
                tops[where, micro] = top
                sums[where, micro] = new_sum
                mixed[where, micro] = new_mixed
                parts[where, micro] = part
                tiles[where, micro] = tile
        return carry

    for pool in range(2):
        if pool == 1:
            for load in loads:
                load.wait()
        count = spots[7, pool * (LANES // 2)]
        steps = (count + together - 1) // together
        lax.fori_loop(0, steps, functools.partial(step, pool), 0)

    pad[:, 0, :] = jnp.sum(tiles[:ranks, 0] + tiles[:ranks, 1], axis=1)
    out_ref[:, heads] = pad[...].astype(BF16)
    out_ref[:, :heads] = parts[:ranks].astype(BF16).reshape(ranks, heads, 2, LANES)


def owner_kernel(heads, scale, part_ref, query_ref, key_ref, value_ref, out_ref, wide):
    count = part_ref.shape[0]
    pieces = heads // 8
    groups = 2 * pieces
    wide[...] = query_ref[...].astype(F32)
    levels = spread_levels(part_ref[:, heads].reshape(2 * count, LANES), groups)
    for g in range(groups):
        micro, piece = g // pieces, g % pieces
        rows = slice(piece * 8, (piece + 1) * 8)
        key = key_ref[micro : micro + 1, :].astype(F32)
        own = jnp.sum(wide[rows, micro, :] * key, axis=1, keepdims=True) * scale
        level = levels[g].reshape(count, 8, LANES)
        top = jnp.maximum(jnp.max(level, axis=0), own)
        weight = jnp.exp(level - top[None])
        self_weight = jnp.exp(own - top)
        part = part_ref[:, 4 * g : 4 * (g + 1)].reshape(8 * count, LANES).astype(F32)
        mixed = jnp.sum(weight * part.reshape(count, 8, LANES), axis=0)
        mixed = mixed + self_weight * value_ref[micro : micro + 1, :].astype(F32)
        wide[rows, micro, :] = mixed / (jnp.sum(weight, axis=0) + self_weight)
    out_ref[...] = wide[...].astype(BF16)


def in_hbm(x):
    return pltpu.with_memory_space_constraint(x, pltpu.HBM)


def in_vmem(x):
    return pltpu.with_memory_space_constraint(x, pltpu.VMEM)


def exchange(x, axis):
    return lax.all_to_all(x, axis, 0, 0)


def per_device(
    queries, new_token_keys, new_token_values, key_pool, value_pool, block_list, context_len
):
    planes, tensor = lax.axis_size("zy"), lax.axis_size("tp")
    micros, _, width = queries.shape
    slots, block_len, dim = key_pool.shape
    heads = width // dim
    scale = dim ** (-0.5)
    per = slots // tensor
    swap = [(0, 1), (1, 0)]
    hbm = pl.BlockSpec(memory_space=pltpu.HBM)
    vmem = pl.BlockSpec(memory_space=pltpu.VMEM)
    params = pltpu.CompilerParams(vmem_limit_bytes=32 * 1024 * 1024)
    message = jax.ShapeDtypeStruct((planes, heads + 1, micros, LANES), BF16)
    query = queries.reshape(micros, heads, dim).transpose(1, 0, 2)

    with jax.named_scope("queries_to_holders"):
        listed, lengths = block_list.transpose(0, 2, 1), context_len.transpose(1, 0)
        copies, ordered, tails = pl.pallas_call(
            functools.partial(first_kernel, (slots // micros - 1) * block_len),
            out_shape=(
                jax.ShapeDtypeStruct((tensor, *listed.shape), jnp.int32),
                jax.ShapeDtypeStruct(query.shape, BF16),
                jax.ShapeDtypeStruct((8, LANES), F32),
            ),
            in_specs=[hbm] * 3,
            out_specs=(vmem,) * 3,
            scratch_shapes=[
                pltpu.VMEM(query.shape, BF16),
                pltpu.VMEM(listed.shape, jnp.int32),
                pltpu.VMEM(lengths.shape, jnp.int32),
                pltpu.VMEM(query.shape, F32),
                pltpu.VMEM((8, LANES), F32),
                pltpu.SemaphoreType.DMA((3,)),
            ],
            compiler_params=params,
        )(in_hbm(query), in_hbm(listed), in_hbm(lengths))
        packed = pl.pallas_call(
            pack_kernel,
            out_shape=message,
            in_specs=[vmem] * 3,
            out_specs=vmem,
            scratch_shapes=[pltpu.VMEM((2 * tensor * micros, LANES), F32)],
            compiler_params=params,
        )(ordered, exchange(copies, "tp"), tails)
        own = exchange(packed, "zy")
    with jax.named_scope("pools_of_both_cores"):
        sib_key = lax.ppermute(key_pool, "c", swap)
        sib_value = lax.ppermute(value_pool, "c", swap)
    with jax.named_scope("block_attention"):
        me = (lax.axis_index("zy") * 2 + lax.axis_index("c")).astype(jnp.int32).reshape(1)
        found = pl.pallas_call(
            functools.partial(find_kernel, tensor, per, block_len),
            out_shape=jax.ShapeDtypeStruct((8, LANES), jnp.int32),
            in_specs=[pl.BlockSpec(memory_space=pltpu.SMEM), vmem],
            out_specs=vmem,
            scratch_shapes=[pltpu.VMEM((planes, 2, LANES), F32)],
            compiler_params=params,
            cost_estimate=pl.CostEstimate(
                flops=COST, bytes_accessed=2 * own.size, transcendentals=0
            ),
        )(me, own)
        parts = pl.pallas_call(
            functools.partial(holder_kernel, heads, scale),
            out_shape=message,
            in_specs=[vmem] * 2 + [hbm] * 2 + [vmem] * 2,
            out_specs=vmem,
            scratch_shapes=[
                pltpu.VMEM(key_pool.shape, BF16),
                pltpu.VMEM(value_pool.shape, BF16),
                *[pltpu.VMEM((planes + 1, micros, heads, LANES), F32)] * 4,
                pltpu.VMEM((planes + 1, micros, 8, LANES), F32),
                pltpu.VMEM((planes, 2, LANES), F32),
                pltpu.SMEM((8, LANES), jnp.int32),
                pltpu.SemaphoreType.DMA((2,)),
                pltpu.SemaphoreType.DMA,
            ],
            compiler_params=params,
        )(own, found, in_hbm(key_pool), in_hbm(value_pool), in_vmem(sib_key), in_vmem(sib_value))
    with jax.named_scope("parts_to_owners"):
        arrived = exchange(parts, "zy")
    with jax.named_scope("owner_sum"):
        out = pl.pallas_call(
            functools.partial(owner_kernel, heads, scale),
            out_shape=jax.ShapeDtypeStruct(query.shape, BF16),
            in_specs=[vmem] * 4,
            out_specs=vmem,
            scratch_shapes=[
                pltpu.VMEM(query.shape, F32),
            ],
            compiler_params=params,
        )(arrived, query, new_token_keys.reshape(micros, dim), new_token_values.reshape(micros, dim))
        return out.transpose(1, 0, 2).reshape(micros, 1, width)


def solution(mesh):
    spread, tensor = mesh.devices.shape
    finer = Mesh(mesh.devices.reshape(spread // 2, 2, tensor), ("zy", "c", "tp"))
    dp = ("zy", "c")
    placed = (
        P(None, dp, "tp"),
        P(None, dp, "tp"),
        P(None, dp, "tp"),
        P(dp, None, "tp"),
        P(dp, None, "tp"),
        P(None, ("zy", "c", "tp"), None),
        P(None, dp),
    )
    return jax.shard_map(
        per_device, mesh=finer, in_specs=placed, out_specs=P(None, dp, "tp"), check_vma=False
    )
```

```python
import functools

import jax
import jax.numpy as jnp
from jax import lax
from jax.experimental import pallas as pl
from jax.experimental.pallas import tpu as pltpu
from jax.sharding import Mesh, PartitionSpec as P

LANES = 128
COST = 10**11
FIELD = 16
SPAN = 32
EMPTY = -1e30
PARTS = 3
F32, BF16 = jnp.float32, jnp.bfloat16


def lane_ids(shape):
    return lax.broadcasted_iota(jnp.int32, shape, len(shape) - 1)


def split3(x):
    high = x.astype(BF16).astype(F32)
    rest = x - high
    middle = rest.astype(BF16).astype(F32)
    return high, middle, rest - middle


def spread_levels(rows, groups):
    count = rows.shape[0] // 2
    line = lax.broadcasted_iota(jnp.int32, (8 * count, 2 * count), 0)
    source = lax.broadcasted_iota(jnp.int32, (8 * count, 2 * count), 1)
    pick = (source == (line // 8) * 2).astype(F32).astype(BF16)
    copies = jnp.dot(pick, rows, preferred_element_type=F32)
    sublane = lax.broadcasted_iota(jnp.int32, copies.shape, 0) % 8
    copies = jnp.where(lane_ids(copies.shape) // FIELD == sublane, copies, 0.0).astype(BF16)
    at = lax.broadcasted_iota(jnp.int32, (LANES, groups * LANES), 0) % FIELD // PARTS
    group = lane_ids((LANES, groups * LANES)) // LANES
    add = (at == group).astype(F32).astype(BF16)
    levels = jnp.dot(copies, add, preferred_element_type=F32)
    return [levels[:, g * LANES : (g + 1) * LANES] for g in range(groups)]


def first_kernel(
    first_tail, query_hbm, list_hbm, length_hbm, copies_ref, query_ref, tail_ref,
    narrow, entries, lengths, wide, rows, sems,
):
    heads, micros, _ = narrow.shape
    loads = [
        pltpu.make_async_copy(list_hbm, entries, sems.at[0]),
        pltpu.make_async_copy(query_hbm, narrow, sems.at[1]),
        pltpu.make_async_copy(length_hbm, lengths, sems.at[2]),
    ]
    for load in loads:
        load.start()
    rows[...] = jnp.zeros(rows.shape, F32)
    loads[0].wait()
    copies_ref[...] = jnp.broadcast_to(entries[...][None], copies_ref.shape)
    loads[1].wait()
    wide[...] = narrow[...].astype(F32)
    query = jnp.concatenate([wide[:, m, :] for m in range(micros)], axis=0).astype(BF16)
    query_ref[...] = query.reshape(heads, micros, LANES)
    loads[2].wait()
    rows[0:1, :micros] = (lengths[...] - first_tail).astype(F32)
    tail_ref[...] = rows[...]


def pack_kernel(query_ref, list_ref, tail_ref, out_ref, rows):
    tensor, micros, _, part = list_ref.shape
    rows[...] = jnp.zeros(rows.shape, F32)
    fields = []
    for t in range(tensor):
        for m in range(micros):
            at = 2 * (t * micros + m)
            rows[at : at + 2, :part] = list_ref[t, m].astype(F32)
            fields.extend((at + field, t * SPAN + field * FIELD + m * part) for field in range(2))
    entries = rows[0:1, :]
    for line, shift in fields[1:]:
        entries = entries + pltpu.roll(rows[line : line + 1, :], shift, 1)
    listed = jnp.concatenate([entries, tail_ref[0:1, :]], axis=0).astype(BF16)
    message = jnp.concatenate([query_ref[...], listed[None]], axis=0)
    out_ref[...] = jnp.broadcast_to(message[None], out_ref.shape)


def find_kernel(tensor, per, block_len, me, own_ref, found_ref, pad):
    ranks, heads = own_ref.shape[0], own_ref.shape[1] - 1
    entries = tensor * per
    per_micro = entries // 2
    lane = lane_ids((ranks, LANES))
    pad[...] = own_ref[:, heads].astype(F32)
    listed = pad[:, 0, :]
    tails = pad[:, 1, :]
    index = lane % FIELD
    order = (index // (per // 2)) * per_micro + (lane // SPAN) * (per // 2) + index % (per // 2)
    place = (lane % SPAN < per) & (lane < tensor * SPAN)
    slot = pltpu.roll(listed, LANES - FIELD, 1)
    code = slot * entries + order.astype(F32)
    firsts, lasts = [], []
    for holder in (me[0] + 1 - 2 * (me[0] % 2), me[0]):
        here = (listed == holder.astype(F32)) & place
        firsts.append(jnp.min(jnp.where(here, code, 1e6), axis=1, keepdims=True))
        lasts.append(jnp.max(jnp.where(here, code, -1.0), axis=1, keepdims=True))
    second = lane >= LANES // 2
    first = jnp.where(second, firsts[1], firsts[0])
    last = jnp.where(second, lasts[1], lasts[0])
    valid = last >= 0.0
    row = lax.broadcasted_iota(jnp.int32, (ranks, ranks), 0)
    ahead = lax.broadcasted_iota(jnp.int32, (ranks, ranks), 1)
    before = jnp.dot(
        (ahead < row).astype(F32).astype(BF16),
        valid.astype(F32).astype(BF16),
        preferred_element_type=F32,
    )
    chosen = valid & (before == (lane % (LANES // 2)).astype(F32))
    rank = lax.broadcasted_iota(jnp.int32, (ranks, LANES), 0).astype(F32)
    tail0 = jnp.sum(jnp.where(lane == 0, tails, 0.0), axis=1, keepdims=True)
    tail1 = jnp.sum(jnp.where(lane == 1, tails, 0.0), axis=1, keepdims=True)

    def listing(x):
        return jnp.sum(jnp.where(chosen, x, 0.0), axis=0, keepdims=True)

    lines = [listing(x) for x in (rank, first, last, tail0, tail1)]
    lines[0] = jnp.where(listing(1.0) > 0.0, lines[0], float(ranks))
    lines.append(jnp.sum(valid.astype(F32), axis=0, keepdims=True))
    ranked, code_a, code_b, left0, left1, count = (x.astype(jnp.int32) for x in lines)
    places, micros, lives = [], [], []
    for code in (code_a, code_b):
        at = code % entries
        micro = at // per_micro
        left = jnp.where(micro == 0, left0, left1)
        places.append(code // entries)
        micros.append(micro)
        lives.append(jnp.where(at % per_micro == per_micro - 1, left, block_len))
    found_ref[...] = jnp.concatenate([ranked, *places, *micros, *lives, count], axis=0)


def holder_kernel(
    heads, scale, own_ref, found_ref, key_ref, value_ref, sib_key_ref, sib_value_ref,
    out_ref, keys, values, tops, sums, mixed, parts, tiles, pad, spots, sems, spot_sem,
):
    ranks = own_ref.shape[0]
    slots, block_len, _ = keys.shape
    groups = 2 * heads // 8
    move = pltpu.make_async_copy(found_ref, spots, spot_sem)
    move.start()
    loads = [
        pltpu.make_async_copy(key_ref, keys, sems.at[0]),
        pltpu.make_async_copy(value_ref, values, sems.at[1]),
    ]
    for load in loads:
        load.start()
    pools = ((sib_key_ref, sib_value_ref), (keys, values))
    tops[...] = jnp.full(tops.shape, EMPTY, F32)
    sums[...] = jnp.zeros(sums.shape, F32)
    mixed[...] = jnp.zeros(mixed.shape, F32)
    parts[...] = jnp.zeros(parts.shape, BF16)
    pad[...] = jnp.zeros(pad.shape, F32)
    lane8 = lane_ids((8, LANES))
    sublane = lax.broadcasted_iota(jnp.int32, (8, LANES), 0)
    field = jnp.where(lane8 // FIELD == sublane, lane8 % FIELD, FIELD)
    half = PARTS * groups // 2
    for micro in range(2):
        blank = jnp.where((field >= micro * half) & (field < (micro + 1) * half), EMPTY, 0.0)
        tiles[:, micro] = jnp.broadcast_to(blank[None], (ranks + 1, 8, LANES))
    move.wait()

    together = min(10, slots // 2)
    token = lane_ids((heads, block_len))

    def step(pool, i, carry):
        work = []
        for k in range(together):
            n = pool * (LANES // 2) + i * together + k
            where = spots[0, n]
            for line in range(2):
                work.append((where, spots[1 + line, n], spots[3 + line, n], spots[5 + line, n]))
        scores = []
        for k in range(together):
            pair = work[2 * k : 2 * k + 2]
            queries = []
            for where, block, micro, live in pair:
                inner = pl.ds(micro * (heads // 2), heads // 2)
                query = own_ref[jnp.minimum(where, ranks - 1), inner].reshape(heads, LANES)
                queries.append(query)
            both = lax.dot_general(
                jnp.concatenate(queries, axis=0),
                jnp.concatenate([pools[pool][0][block] for _, block, _, _ in pair], axis=0),
                (((1,), (1,)), ((), ())),
                preferred_element_type=F32,
            )
            for line, (where, block, micro, live) in enumerate(pair):
                score = both[line * heads : (line + 1) * heads, line * block_len : (line + 1) * block_len]
                scores.append(jnp.where(token < live, score * scale, EMPTY))
        score = jnp.concatenate(scores, axis=0)
        peak = jnp.max(score, axis=1, keepdims=True)
        weight = jnp.exp(score - peak)
        total = jnp.sum(weight, axis=1, keepdims=True)
        weight = weight.astype(BF16)
        nothing = jnp.zeros((heads, block_len), BF16)
        mixes = []
        for k in range(together):
            wa = weight[2 * k * heads : (2 * k + 1) * heads]
            wb = weight[(2 * k + 1) * heads : (2 * k + 2) * heads]
            spread = jnp.concatenate(
                [
                    jnp.concatenate([wa, nothing], axis=1),
                    jnp.concatenate([nothing, wb], axis=1),
                ],
                axis=0,
            )
            pair = jnp.concatenate(
                [pools[pool][1][work[2 * k][1]], pools[pool][1][work[2 * k + 1][1]]], axis=0
            )
            mixes.append(jnp.dot(spread, pair, preferred_element_type=F32))
        for line in range(2):
            olds = []
            for where, block, micro, live in work[line::2]:
                olds.append((tops[where, micro], sums[where, micro], mixed[where, micro]))
            news = []
            for k, (where, block, micro, live) in enumerate(work[line::2]):
                rows = slice((2 * k + line) * heads, (2 * k + line + 1) * heads)
                part = mixes[k][line * heads : (line + 1) * heads]
                old_top, old_sum, old_mixed = olds[k]
                top = jnp.maximum(old_top, peak[rows])
                old_scale, scale_here = jnp.exp(old_top - top), jnp.exp(peak[rows] - top)
                new_sum = old_scale * old_sum + scale_here * total[rows]
                new_mixed = old_scale * old_mixed + scale_here * part
                depth = top + jnp.log(new_sum)
                tile = jnp.zeros((8, LANES), F32)
                for piece in range(heads // 8):
                    for j, term in enumerate(split3(depth[piece * 8 : (piece + 1) * 8])):
                        tile = jnp.where(field == PARTS * piece + j + micro * half, term, tile)
                news.append((where, micro, top, new_sum, new_mixed, new_mixed / new_sum, tile))
            for where, micro, top, new_sum, new_mixed, part, tile in news:
                tops[where, micro] = top
                sums[where, micro] = new_sum
                mixed[where, micro] = new_mixed
                inner = pl.ds(micro * (heads // 2), heads // 2)
                parts[where, inner] = part.astype(BF16).reshape(heads // 2, 2, LANES)
                tiles[where, micro] = tile
        return carry

    for pool in range(2):
        if pool == 1:
            for load in loads:
                load.wait()
        count = spots[7, pool * (LANES // 2)]
        steps = (count + together - 1) // together
        lax.fori_loop(0, steps, functools.partial(step, pool), 0)

    pad[:, 0, :] = jnp.sum(tiles[:ranks, 0] + tiles[:ranks, 1], axis=1)
    out_ref[:, heads] = pad[...].astype(BF16)
    out_ref[:, :heads] = parts[:ranks]


def owner_kernel(heads, scale, part_ref, query_ref, key_ref, value_ref, out_ref, wide):
    count = part_ref.shape[0]
    pieces = heads // 8
    groups = 2 * pieces
    wide[...] = query_ref[...].astype(F32)
    levels = spread_levels(part_ref[:, heads].reshape(2 * count, LANES), groups)
    for g in range(groups):
        micro, piece = g // pieces, g % pieces
        rows = slice(piece * 8, (piece + 1) * 8)
        key = key_ref[micro : micro + 1, :].astype(F32)
        own = jnp.sum(wide[rows, micro, :] * key, axis=1, keepdims=True) * scale
        level = levels[g].reshape(count, 8, LANES)
        top = jnp.maximum(jnp.max(level, axis=0), own)
        weight = jnp.exp(level - top[None])
        self_weight = jnp.exp(own - top)
        part = part_ref[:, 4 * g : 4 * (g + 1)].reshape(8 * count, LANES).astype(F32)
        mixed = jnp.sum(weight * part.reshape(count, 8, LANES), axis=0)
        mixed = mixed + self_weight * value_ref[micro : micro + 1, :].astype(F32)
        wide[rows, micro, :] = mixed / (jnp.sum(weight, axis=0) + self_weight)
    out_ref[...] = wide[...].astype(BF16)


def in_hbm(x):
    return pltpu.with_memory_space_constraint(x, pltpu.HBM)


def in_vmem(x):
    return pltpu.with_memory_space_constraint(x, pltpu.VMEM)


def exchange(x, axis):
    return lax.all_to_all(x, axis, 0, 0)


def per_device(
    queries, new_token_keys, new_token_values, key_pool, value_pool, block_list, context_len
):
    planes, tensor = lax.axis_size("zy"), lax.axis_size("tp")
    micros, _, width = queries.shape
    slots, block_len, dim = key_pool.shape
    heads = width // dim
    scale = dim ** (-0.5)
    per = slots // tensor
    swap = [(0, 1), (1, 0)]
    hbm = pl.BlockSpec(memory_space=pltpu.HBM)
    vmem = pl.BlockSpec(memory_space=pltpu.VMEM)
    params = pltpu.CompilerParams(vmem_limit_bytes=32 * 1024 * 1024)
    message = jax.ShapeDtypeStruct((planes, heads + 1, micros, LANES), BF16)
    query = queries.reshape(micros, heads, dim).transpose(1, 0, 2)

    with jax.named_scope("queries_to_holders"):
        listed, lengths = block_list.transpose(0, 2, 1), context_len.transpose(1, 0)
        copies, ordered, tails = pl.pallas_call(
            functools.partial(first_kernel, (slots // micros - 1) * block_len),
            out_shape=(
                jax.ShapeDtypeStruct((tensor, *listed.shape), jnp.int32),
                jax.ShapeDtypeStruct(query.shape, BF16),
                jax.ShapeDtypeStruct((8, LANES), F32),
            ),
            in_specs=[hbm] * 3,
            out_specs=(vmem,) * 3,
            scratch_shapes=[
                pltpu.VMEM(query.shape, BF16),
                pltpu.VMEM(listed.shape, jnp.int32),
                pltpu.VMEM(lengths.shape, jnp.int32),
                pltpu.VMEM(query.shape, F32),
                pltpu.VMEM((8, LANES), F32),
                pltpu.SemaphoreType.DMA((3,)),
            ],
            compiler_params=params,
        )(in_hbm(query), in_hbm(listed), in_hbm(lengths))
        packed = pl.pallas_call(
            pack_kernel,
            out_shape=message,
            in_specs=[vmem] * 3,
            out_specs=vmem,
            scratch_shapes=[pltpu.VMEM((2 * tensor * micros, LANES), F32)],
            compiler_params=params,
        )(ordered, exchange(copies, "tp"), tails)
        own = exchange(packed, "zy")
    with jax.named_scope("pools_of_both_cores"):
        sib_key = lax.ppermute(key_pool, "c", swap)
        sib_value = lax.ppermute(value_pool, "c", swap)
    with jax.named_scope("block_attention"):
        me = (lax.axis_index("zy") * 2 + lax.axis_index("c")).astype(jnp.int32).reshape(1)
        found = pl.pallas_call(
            functools.partial(find_kernel, tensor, per, block_len),
            out_shape=jax.ShapeDtypeStruct((8, LANES), jnp.int32),
            in_specs=[pl.BlockSpec(memory_space=pltpu.SMEM), vmem],
            out_specs=vmem,
            scratch_shapes=[pltpu.VMEM((planes, 2, LANES), F32)],
            compiler_params=params,
            cost_estimate=pl.CostEstimate(
                flops=COST, bytes_accessed=2 * own.size, transcendentals=0
            ),
        )(me, own)
        parts = pl.pallas_call(
            functools.partial(holder_kernel, heads, scale),
            out_shape=message,
            in_specs=[vmem] * 2 + [hbm] * 2 + [vmem] * 2,
            out_specs=vmem,
            scratch_shapes=[
                pltpu.VMEM(key_pool.shape, BF16),
                pltpu.VMEM(value_pool.shape, BF16),
                *[pltpu.VMEM((planes + 1, micros, heads, LANES), F32)] * 3,
                pltpu.VMEM((planes + 1, heads, micros, LANES), BF16),
                pltpu.VMEM((planes + 1, micros, 8, LANES), F32),
                pltpu.VMEM((planes, 2, LANES), F32),
                pltpu.SMEM((8, LANES), jnp.int32),
                pltpu.SemaphoreType.DMA((2,)),
                pltpu.SemaphoreType.DMA,
            ],
            compiler_params=params,
        )(own, found, in_hbm(key_pool), in_hbm(value_pool), in_vmem(sib_key), in_vmem(sib_value))
    with jax.named_scope("parts_to_owners"):
        arrived = exchange(parts, "zy")
    with jax.named_scope("owner_sum"):
        out = pl.pallas_call(
            functools.partial(owner_kernel, heads, scale),
            out_shape=jax.ShapeDtypeStruct(query.shape, BF16),
            in_specs=[vmem] * 4,
            out_specs=vmem,
            scratch_shapes=[
                pltpu.VMEM(query.shape, F32),
            ],
            compiler_params=params,
        )(arrived, query, new_token_keys.reshape(micros, dim), new_token_values.reshape(micros, dim))
        return out.transpose(1, 0, 2).reshape(micros, 1, width)


def solution(mesh):
    spread, tensor = mesh.devices.shape
    finer = Mesh(mesh.devices.reshape(spread // 2, 2, tensor), ("zy", "c", "tp"))
    dp = ("zy", "c")
    placed = (
        P(None, dp, "tp"),
        P(None, dp, "tp"),
        P(None, dp, "tp"),
        P(dp, None, "tp"),
        P(dp, None, "tp"),
        P(None, ("zy", "c", "tp"), None),
        P(None, dp),
    )
    return jax.shard_map(
        per_device, mesh=finer, in_specs=placed, out_specs=P(None, dp, "tp"), check_vma=False
    )
```
